32 devices in a mesh: grp: 2 (over y), inst: 8 (over z, x), tp: 2 (over core).
Axes of the slice: x: 2, y: 2, z: 4, core: 2. Of those that a mesh axis runs over, the one named last changes fastest.
Arguments:
- queries: bfloat16 [8192, 12288], P(('grp', 'inst'), 'tp'), parts along dimension 0, may hold values from -330 to 330
- keys_values: bfloat16 [8192, 2048], P(('grp', 'inst')), parts along dimension 0, may hold values from -5 to 5
- out_weight: bfloat16 [12288, 12288], P('tp', 'inst'), may hold values from -0.0546875 to 0.0546875
- lengths: int32 [16, 4], P(('grp', 'inst')), parts along dimension 0, may hold values from 1 to 256, 512 in all within a row
- placement: int32 [64], P('grp'), parts along dimension 0, may hold values from 0 to 1
- page_table: int32 [64, 16], P('grp'), parts along dimension 0, may hold values from 0 to 127, as said below
Outputs:
- projected: bfloat16 [8192, 12288], P(('grp', 'inst', 'tp')), parts along dimension 0
- cache: bfloat16 [2048, 16, 2048], P(('grp', 'inst'), None, 'tp'), parts along dimension 0
The draws below stay inside these ranges and needn't reach their ends.
There are 2 independent parts, one for each index of `grp`. The reference program is written for one: setup_inputs(seed, part) draws one part's arguments, and reference() takes and returns one part's arrays. A program takes and returns all parts, laid end to end along the dimension named above; an argument that names none is the same for every part. Nothing has to cross between parts.
Inputs may be any that keep to these rules, and one draw needn't show every extreme that they name: `page_table`: pages of different requests, or of different p // 4, with equal p % 4 hold different slots.
All inputs are finite; a program needn't handle non-finite values.
Results may differ from the reference program's by a relative error of at most 0.013.
Values may be sent and summed in bfloat16 or wider, within the bound.
No kernel may reach another device: no remote copies, remote signals or barrier semaphores. Data moves between devices by JAX's collectives and lax.ppermute only.
A program may use at most 512 MiB of HBM per device.

```python
import math
import jax
import jax.numpy as jnp
import numpy as np
from jax import lax

D = 12288
NH = 96
KVH = 8
HD = 128
PAGE = 16
OWNERS = 4
REQ_INST = 4
TOK_INST = 512
MAXLEN = 256
MAXPAGES = 16
QUARTERS = 4
REQS = 32
SLOTS = 128
TOKENS = 4096
N_INST = 8
N_TP = 2


def shared_pairs(key):
    base = jnp.clip(jax.random.normal(key, (TOKENS, KVH, 2, HD), jnp.float32), -5.0, 5.0)
    marked = jnp.arange(TOKENS) % 32 == 30
    keys_new = jnp.where(marked[:, None, None], base[:, :, 0], base[:, :, 0])
    return jnp.stack([keys_new, base[:, :, 1]], axis=2)


def draw_keys_values(key, part):
    pairs = shared_pairs(key)
    return pairs.reshape(TOKENS, 2 * KVH * HD).astype(jnp.bfloat16)


def draw_queries(key, part):
    key = jax.random.fold_in(key, 5)
    values = jnp.clip(jax.random.normal(key, (TOKENS, NH, HD), jnp.float32), -5.0, 5.0)
    return values.reshape(TOKENS, NH * HD).astype(jnp.bfloat16)


def draw_page_table(key, part):
    key = jax.random.fold_in(key, 7)
    tables = []
    for residue in range(OWNERS):
        order = jax.random.permutation(jax.random.fold_in(key, residue), REQS * QUARTERS).astype(jnp.int32)
        tables.append(order.reshape(REQS, QUARTERS))
    return jnp.stack(tables, axis=2).reshape(REQS, MAXPAGES).astype(jnp.int32)


def with_ends(array, key, low, high):
    shape = array.shape
    index_at = [jax.random.randint(jax.random.fold_in(key, axis), (), 0, shape[axis]) for axis in range(len(shape))]
    array = array.at[tuple(index_at)].set(low)
    longest = shape.index(max(shape))
    index_at[longest] = (index_at[longest] + 1) % shape[longest]
    return array.at[tuple(index_at)].set(high)


def block_scale(stream_key, shape, split, smallest, top_value):
    factor_of = 1.0
    for position, blocks in split:
        steps = jax.random.uniform(jax.random.fold_in(jax.random.fold_in(stream_key, 6), position), (blocks,), jnp.float32, smallest / len(split), top_value / len(split))
        factor_of = factor_of * jnp.repeat(jnp.exp(steps), shape[position] // blocks).reshape((-1,) + (1,) * (len(shape) - 1 - position))
    return factor_of


def split_up(number_of, total, limit, slope):
    loads = [(1 << 20) // math.isqrt(rank ** slope) + 1 for rank in range(2, number_of + 1)]
    spare, counts = total - limit - (number_of - 1), [1] * (number_of - 1)
    while spare > 0:
        movable = [i for i in range(number_of - 1) if counts[i] < limit]
        mass, left = sum([loads[i] for i in movable]), spare
        for i in movable:
            more = min(limit - counts[i], max(1, left * loads[i] // mass), spare)
            counts[i] = counts[i] + more
            spare = spare - more
    return np.array([limit] + counts)


def ragged_sizes(own_key, amount, total, reach, lean):
    if amount == 2:
        one = jax.random.randint(own_key, (), max(1, total - reach), min(reach, total - 1) + 1)
        return jnp.stack([one, total - one])
    tallies = jnp.asarray(split_up(amount, total, reach, lean), jnp.int32)
    couples = (amount - 1) // 2
    source_of, taker = tallies[1:1 + 2 * couples:2], tallies[2:2 + 2 * couples:2]
    margin = jnp.minimum(source_of - 1, reach - taker)
    passed = jax.random.randint(jax.random.fold_in(own_key, 1), (couples,), 0, 1 << 20) % (margin + 1)
    tallies = tallies.at[1:1 + 2 * couples:2].set(source_of - passed).at[2:2 + 2 * couples:2].set(taker + passed)
    return tallies[jax.random.permutation(jax.random.fold_in(own_key, 2), amount)]


def scatter_about(stream_key, dims, deviation, most, pieces=(), kind=jnp.bfloat16):
    level = block_scale(stream_key, dims, pieces, -0.22, 0.18) if pieces else 1.0
    drawn = jax.random.normal(stream_key, dims, jnp.float32) * deviation * level
    return jnp.minimum(jnp.maximum(drawn, -most), most).astype(kind)


def setup_inputs(seed: int = 0, part: int = 0) -> dict:
    arg_keys = jax.random.split(jax.random.key(seed), 7)
    part_keys = jax.random.split(jax.random.fold_in(arg_keys[6], part), 7)
    queries = draw_queries(jax.random.fold_in(jax.random.fold_in(arg_keys[6], part), 71), part)
    keys_values = draw_keys_values(jax.random.fold_in(jax.random.fold_in(arg_keys[6], part), 71), part)
    out_weight = scatter_about(arg_keys[2], (NH * HD, D), (NH * HD) ** -0.5, 0.0546875, ((0, 2), (1, 8)))
    lengths = jax.vmap(lambda own: ragged_sizes(own, REQ_INST, TOK_INST, MAXLEN, 2))(jax.random.split(part_keys[3], N_INST)).reshape((N_INST, REQ_INST)).astype(jnp.int32)
    placement = with_ends(jax.random.randint(part_keys[4], (REQS,), 0, N_INST // OWNERS), jax.random.fold_in(part_keys[4], 1), 0, (N_INST // OWNERS) - 1).astype(jnp.int32)
    page_table = draw_page_table(jax.random.fold_in(jax.random.fold_in(arg_keys[6], part), 71), part)
    return dict(queries=queries, keys_values=keys_values, out_weight=out_weight, lengths=lengths, placement=placement, page_table=page_table)


def attend(query_rows, pair_rows, lens_row):
    ends = jnp.cumsum(lens_row).astype(jnp.int32)
    positions = jnp.arange(TOK_INST, dtype=jnp.int32)
    segment = jnp.sum((positions[:, None] >= ends[None, :]).astype(jnp.int32), axis=1)
    allowed = (segment[:, None] == segment[None, :]) & (positions[None, :] <= positions[:, None])
    keys_full = jnp.repeat(pair_rows[:, :, 0], NH // KVH, axis=1).astype(jnp.float32)
    vals_full = jnp.repeat(pair_rows[:, :, 1], NH // KVH, axis=1).astype(jnp.float32)
    scores = jnp.einsum("qhd,khd->hqk", query_rows.astype(jnp.float32), keys_full) * (1.0 / (HD ** 0.5))
    scores = jnp.where(allowed[None], scores, -1e30)
    top_score = jnp.max(scores, axis=2, keepdims=True)
    expo = jnp.exp(scores - top_score)
    probs = (expo / jnp.sum(expo, axis=2, keepdims=True)).astype(jnp.bfloat16)
    mixed = jnp.einsum("hqk,khd->qhd", probs.astype(jnp.float32), vals_full)
    return mixed.astype(jnp.bfloat16).reshape(TOK_INST, NH * HD)


def reference(queries, keys_values, out_weight, lengths, placement, page_table):
    kv_cols = 2 * KVH * HD
    group_cols = NH * HD // N_TP
    query_all = queries.reshape(N_INST, TOK_INST, NH, HD)
    pair_all = keys_values.reshape(N_INST, TOK_INST, KVH, 2, HD)
    weight_parts = out_weight.reshape(N_TP, group_cols, D)

    def one_instance(inputs):
        query_rows, pair_rows, lens_row = inputs
        attended = attend(query_rows, pair_rows, lens_row)
        parts = attended.reshape(TOK_INST, N_TP, group_cols).transpose(1, 0, 2)

        def add_part(total, pair):
            piece, weight = pair
            term = jnp.dot(piece, weight, preferred_element_type=jnp.float32).astype(jnp.bfloat16)
            term = lax.optimization_barrier(term)
            return total + term.astype(jnp.float32), None

        total, unused = lax.scan(add_part, jnp.zeros((TOK_INST, D), jnp.float32), (parts, weight_parts))
        return total.astype(jnp.bfloat16)

    projected = lax.map(one_instance, (query_all, pair_all, lengths)).reshape(TOKENS, D)

    lens_flat = lengths.reshape(-1).astype(jnp.int32)
    starts = (jnp.cumsum(lengths, axis=1) - lengths).reshape(-1).astype(jnp.int32)
    inst_of = (jnp.arange(REQS, dtype=jnp.int32) // REQ_INST).astype(jnp.int32)
    offsets = jnp.arange(MAXLEN, dtype=jnp.int32)
    rows = jnp.clip(starts[:, None] + offsets[None, :], 0, TOK_INST - 1) + inst_of[:, None] * TOK_INST
    live = offsets[None, :] < lens_flat[:, None]
    taken = jnp.take(keys_values, rows.reshape(-1).astype(jnp.int32), axis=0).reshape(REQS, MAXLEN, kv_cols)
    padded = jnp.where(live[:, :, None], taken, jnp.zeros_like(taken))
    pages = padded.reshape(REQS * MAXPAGES, PAGE, kv_cols)
    page_index = jnp.arange(MAXPAGES, dtype=jnp.int32)
    owner = OWNERS * placement[:, None] + page_index[None, :] % OWNERS
    target = (owner * SLOTS + page_table).reshape(-1).astype(jnp.int32)
    cache = jnp.zeros((N_INST * SLOTS, PAGE, kv_cols), keys_values.dtype).at[target].set(pages)
    return projected, cache
```

```python
import functools

import jax
import jax.numpy as jnp
from jax import lax
from jax.experimental import pallas as pl
from jax.experimental.pallas import tpu as pltpu
from jax.sharding import PartitionSpec as P

NH = 96
KVH = 8
HD = 128
PAGE = 16
OWNERS = 4
REQ_INST = 4
MAXLEN = 256
QUARTERS = 4
ROWS = 128
LOG2E = 1.4426950408889634

SIDE, NEXT, FAR = 1, 2, 4
PIECES = (256, 256, 128, 128)


def attention_kernel(info, q_ref, k_ref, v_ref, o_ref, *, heads, row_blocks, window):
    for block in range(row_blocks):
        place = info[0] * row_blocks + block
        first = pl.multiple_of(jnp.maximum(place - (window // ROWS - 1), 0) * ROWS, ROWS)
        row = place * ROWS + lax.broadcasted_iota(jnp.int32, (ROWS, window), 0)
        col = first + lax.broadcasted_iota(jnp.int32, (ROWS, window), 1)
        begin = jnp.zeros_like(row)
        for j in range(REQ_INST):
            begin = jnp.where(row >= info[2 + j], info[2 + j], begin)
        bias = jnp.where((col <= row) & (col >= begin), 0.0, -1e30)
        keys = k_ref[pl.ds(first, window), :]
        vals = v_ref[pl.ds(first, window), :]
        vals = jnp.concatenate([vals, jnp.ones_like(vals)], axis=1)
        rows = slice(block * ROWS, (block + 1) * ROWS)
        for head in range(heads):
            cols = slice(head * HD, (head + 1) * HD)
            scores = lax.dot_general(
                q_ref[rows, cols], keys, (((1,), (1,)), ((), ())),
                preferred_element_type=jnp.float32,
            )
            scores = scores * (LOG2E / HD**0.5) + bias
            expo = jnp.exp2(scores - jnp.max(scores, axis=1, keepdims=True))
            mixed = jnp.dot(expo.astype(jnp.bfloat16), vals, preferred_element_type=jnp.float32)
            o_ref[rows, cols] = (mixed[:, :HD] / mixed[:, HD:]).astype(jnp.bfloat16)


def attention(queries, keys_values, ends, first_kv, chunk, chunk_rows):
    tok_rows, width = queries.shape
    local_heads = width // HD
    kv_heads = max(1, local_heads // (NH // KVH))
    heads = local_heads // kv_heads
    window = min(ROWS + MAXLEN, tok_rows)
    info = jnp.concatenate([jnp.stack([chunk, first_kv]).astype(jnp.int32), ends])
    work = chunk_rows * window * width
    return pl.pallas_call(
        functools.partial(
            attention_kernel, heads=heads, row_blocks=chunk_rows // ROWS, window=window
        ),
        grid_spec=pltpu.PrefetchScalarGridSpec(
            num_scalar_prefetch=1,
            grid=(kv_heads,),
            in_specs=[
                pl.BlockSpec((chunk_rows, heads * HD), lambda g, info: (info[0], g)),
                pl.BlockSpec((tok_rows, HD), lambda g, info: (0, 2 * (info[1] + g))),
                pl.BlockSpec((tok_rows, HD), lambda g, info: (0, 2 * (info[1] + g) + 1)),
            ],
            out_specs=pl.BlockSpec((chunk_rows, heads * HD), lambda g, info: (0, g)),
        ),
        out_shape=jax.ShapeDtypeStruct((chunk_rows, width), jnp.bfloat16),
        compiler_params=pltpu.CompilerParams(vmem_limit_bytes=32 << 20),
        cost_estimate=pl.CostEstimate(
            flops=6 * work, bytes_accessed=4 * chunk_rows * width, transcendentals=work // HD
        ),
        name="attention",
    )(info, queries, keys_values, keys_values)


def place_kernel(offsets, *refs, count):
    pieces, out, sems = refs[:count], refs[count], refs[count + 1]
    copies = []
    for n, piece in enumerate(pieces):
        width = piece.shape[1]
        start = pl.multiple_of(offsets[n], 128)
        copies.append(
            pltpu.make_async_copy(piece, out.at[:, pl.ds(start, width)], sems.at[n])
        )
    for copy in copies:
        copy.start()
    for copy in copies:
        copy.wait()


def place(pieces, offsets, columns):
    rows = pieces[0].shape[0]
    return pl.pallas_call(
        functools.partial(place_kernel, count=len(pieces)),
        grid_spec=pltpu.PrefetchScalarGridSpec(
            num_scalar_prefetch=1,
            grid=(),
            in_specs=[pl.BlockSpec(memory_space=pl.ANY)] * len(pieces),
            out_specs=pl.BlockSpec(memory_space=pl.ANY),
            scratch_shapes=[pltpu.SemaphoreType.DMA((len(pieces),))],
        ),
        out_shape=jax.ShapeDtypeStruct((rows, columns), pieces[0].dtype),
        cost_estimate=pl.CostEstimate(
            flops=0, bytes_accessed=4 * rows * columns, transcendentals=0
        ),
        name="place",
    )(jnp.stack(offsets).astype(jnp.int32), *pieces)


def hop(array, mask):
    count = lax.axis_size("inst")
    return lax.ppermute(array, "inst", [(i, i ^ mask) for i in range(count)])


def swap(array, axis):
    return lax.ppermute(array, axis, [(0, 1), (1, 0)])


def dot(left, right):
    return jnp.dot(left, right, preferred_element_type=jnp.float32)


def group_sum(parts, weight):
    if lax.axis_size("tp") == 2:
        given, kept = parts
        other = swap(dot(given, weight).astype(jnp.bfloat16), "tp")
        return (dot(kept, weight) + other.astype(jnp.float32)).astype(jnp.bfloat16)
    (rows,) = parts
    term = dot(rows, weight).astype(jnp.bfloat16)
    return lax.psum_scatter(term, "tp", scatter_dimension=0, tiled=True)


def fill_cache(keys_values, lengths, placement, page_table):
    tok_rows = keys_values.shape[0]
    tp_count = lax.axis_size("tp")
    inst_count = lax.axis_size("inst")
    inst_here = lax.axis_index("inst")
    kv_width = keys_values.shape[1] // tp_count
    held = lax.dynamic_slice_in_dim(keys_values, lax.axis_index("tp") * kv_width, kv_width, 1)
    for mask in (FAR, NEXT, SIDE):
        held = jnp.concatenate([held, hop(held, mask)], axis=0)
    order = [0]
    for mask in (FAR, NEXT, SIDE):
        order = order + [at ^ mask for at in order]
    block_of = jnp.asarray([order.index(i) for i in range(inst_count)], jnp.int32)

    lens = lax.all_gather(lengths, "inst", axis=0, tiled=True)
    starts = jnp.cumsum(lens, axis=1) - lens
    requests = page_table.shape[0]
    slot_count = requests * QUARTERS
    residue = inst_here % OWNERS
    slots = lax.dynamic_index_in_dim(
        page_table.reshape(requests, QUARTERS, OWNERS), residue, axis=2, keepdims=False
    )
    valid = placement == inst_here // OWNERS
    target = jnp.where(valid[:, None], slots, slot_count).reshape(-1)
    inst_of = jnp.arange(requests, dtype=jnp.int32) // REQ_INST
    base = jnp.take(block_of, inst_of ^ inst_here) * tok_rows + starts.reshape(-1)
    offset = (jnp.arange(QUARTERS, dtype=jnp.int32) * OWNERS + residue) * PAGE
    page_base = (base[:, None] + offset[None, :]).reshape(-1)
    page_live = jnp.clip(lens.reshape(-1)[:, None] - offset[None, :], 0, PAGE).reshape(-1)
    match = target[None, :] == jnp.arange(slot_count, dtype=jnp.int32)[:, None]
    slot_base = jnp.sum(jnp.where(match, page_base[None, :], 0), axis=1)
    slot_live = jnp.sum(jnp.where(match, page_live[None, :], 0), axis=1)
    within = jnp.arange(PAGE, dtype=jnp.int32)
    live = within[None, :] < slot_live[:, None]
    rows = jnp.where(live, slot_base[:, None] + within[None, :], 0)
    taken = jnp.take(held, rows.reshape(-1), axis=0, mode="clip")
    taken = taken.reshape(slot_count, PAGE, kv_width)
    return jnp.where(live[:, :, None], taken, jnp.zeros_like(taken))


def per_device(queries, keys_values, out_weight, lengths, placement, page_table):
    tok_rows = queries.shape[0]
    tp_count = lax.axis_size("tp")
    tp_here = lax.axis_index("tp")
    inst_count = lax.axis_size("inst")
    inst_here = lax.axis_index("inst")
    grp_here = lax.axis_index("grp")
    local_heads = queries.shape[1] // HD
    first_kv = tp_here * local_heads // (NH // KVH)
    ends = jnp.cumsum(lengths[0])
    depth, own_cols = out_weight.shape
    half_cols = own_cols // 2

    chunks = [1 - tp_here, tp_here] if tp_count == 2 else [jnp.int32(0)]
    chunk_rows = tok_rows // len(chunks)
    attended = [
        attention(queries, keys_values, ends, first_kv, chunk, chunk_rows) for chunk in chunks
    ]
    blocks = {0: attended}
    blocks[NEXT] = [hop(rows, NEXT) for rows in attended]
    blocks[SIDE] = [hop(rows, SIDE) for rows in attended]
    blocks[NEXT | SIDE] = [hop(rows, SIDE) for rows in blocks[NEXT]]
    masks = (0, NEXT, SIDE, NEXT | SIDE)

    arrived = []
    at = 0
    for n, width in enumerate(PIECES):
        piece = lax.dynamic_slice(
            out_weight, (jnp.int32(0), grp_here * half_cols + at), (depth, width)
        )
        if n >= 2:
            piece, _ = lax.optimization_barrier((piece, arrived[n - 2][0]))
        along = hop(piece, FAR)
        arrived.append((along, swap(along, "grp"), at, width))
        at += width

    pieces, offsets = [], []

    def hand_out(shares, column_of):
        for mask in masks:
            share = shares[mask]
            pieces.append(hop(share, mask) if mask else share)
            offsets.append(column_of(inst_here ^ mask))

    hand_out(
        {mask: group_sum(blocks[mask], out_weight) for mask in masks},
        lambda inst: inst * own_cols,
    )
    stacked = [
        jnp.concatenate([blocks[mask][c] for mask in masks], axis=0) for c in range(len(chunks))
    ]
    rows_dev = tok_rows // tp_count
    for along, across, at, width in arrived:
        for weight, half in ((along, grp_here), (across, 1 - grp_here)):
            if tp_count == 2:
                total = group_sum(stacked, weight)
                shares = {
                    mask: total[n * rows_dev : (n + 1) * rows_dev] for n, mask in enumerate(masks)
                }
            else:
                shares = {mask: group_sum(blocks[mask], weight) for mask in masks}
            hand_out(
                shares,
                lambda inst, half=half, at=at: (inst ^ FAR) * own_cols + half * half_cols + at,
            )
    projected = place(pieces, offsets, inst_count * own_cols)
    cache = fill_cache(keys_values, lengths, placement, page_table)
    return (projected, cache)


def solution(mesh):
    return jax.shard_map(
        per_device,
        mesh=mesh,
        in_specs=(
            P(("grp", "inst"), "tp"),
            P(("grp", "inst"), None),
            P("tp", "inst"),
            P(("grp", "inst"), None),
            P("grp"),
            P("grp", None),
        ),
        out_specs=(P(("grp", "inst", "tp"), None), P(("grp", "inst"), None, "tp")),
        check_vma=False,
    )
```

```python
import functools

import jax
import jax.numpy as jnp
from jax import lax
from jax.experimental import pallas as pl
from jax.experimental.pallas import tpu as pltpu
from jax.sharding import PartitionSpec as P

NH = 96
KVH = 8
HD = 128
PAGE = 16
OWNERS = 4
REQ_INST = 4
MAXLEN = 256
QUARTERS = 4
ROWS = 128
LOG2E = 1.4426950408889634

SIDE, NEXT, FAR = 1, 2, 4
MASKS = (0, NEXT, SIDE, NEXT | SIDE)
WIDTH = 128
LIGHT = pl.CostEstimate(flops=0, bytes_accessed=0, transcendentals=0)


def attention_kernel(info, q_ref, k_ref, v_ref, o_ref, *, heads, row_blocks, window):
    for block in range(row_blocks):
        place = info[0] * row_blocks + block
        first = pl.multiple_of(jnp.maximum(place - (window // ROWS - 1), 0) * ROWS, ROWS)
        row = place * ROWS + lax.broadcasted_iota(jnp.int32, (ROWS, window), 0)
        col = first + lax.broadcasted_iota(jnp.int32, (ROWS, window), 1)
        begin = jnp.zeros_like(row)
        for j in range(REQ_INST):
            begin = jnp.where(row >= info[2 + j], info[2 + j], begin)
        bias = jnp.where((col <= row) & (col >= begin), 0.0, -1e30)
        keys = k_ref[pl.ds(first, window), :]
        vals = v_ref[pl.ds(first, window), :]
        vals = jnp.concatenate([vals, jnp.ones_like(vals)], axis=1)
        rows = slice(block * ROWS, (block + 1) * ROWS)
        for head in range(heads):
            cols = slice(head * HD, (head + 1) * HD)
            scores = lax.dot_general(
                q_ref[rows, cols], keys, (((1,), (1,)), ((), ())),
                preferred_element_type=jnp.float32,
            )
            scores = scores * (LOG2E / HD**0.5) + bias
            expo = jnp.exp2(scores - jnp.max(scores, axis=1, keepdims=True))
            mixed = jnp.dot(expo.astype(jnp.bfloat16), vals, preferred_element_type=jnp.float32)
            o_ref[rows, cols] = (mixed[:, :HD] / mixed[:, HD:]).astype(jnp.bfloat16)


def attention(queries, keys_values, ends, first_kv, chunk, chunk_rows, part, parts):
    tok_rows, width = queries.shape
    local_heads = width // HD
    kv_heads = max(1, local_heads // (NH // KVH))
    heads = local_heads // kv_heads
    steps = kv_heads // parts
    window = min(ROWS + MAXLEN, tok_rows)
    first_kv = first_kv + part * steps
    info = jnp.concatenate([jnp.stack([chunk, first_kv]).astype(jnp.int32), ends])
    return pl.pallas_call(
        functools.partial(
            attention_kernel, heads=heads, row_blocks=chunk_rows // ROWS, window=window
        ),
        grid_spec=pltpu.PrefetchScalarGridSpec(
            num_scalar_prefetch=1,
            grid=(steps,),
            in_specs=[
                pl.BlockSpec(
                    (chunk_rows, heads * HD), lambda g, info: (info[0], part * steps + g)
                ),
                pl.BlockSpec((tok_rows, HD), lambda g, info: (0, 2 * (info[1] + g))),
                pl.BlockSpec((tok_rows, HD), lambda g, info: (0, 2 * (info[1] + g) + 1)),
            ],
            out_specs=pl.BlockSpec((chunk_rows, heads * HD), lambda g, info: (0, g)),
        ),
        out_shape=jax.ShapeDtypeStruct((chunk_rows, width // parts), jnp.bfloat16),
        compiler_params=pltpu.CompilerParams(vmem_limit_bytes=32 << 20),
        cost_estimate=LIGHT,
        name="attention",
    )(info, queries, keys_values, keys_values)


def place_kernel(offsets, *refs, segments):
    out = refs[-1]
    for n, (source, at, width) in enumerate(segments):
        start = pl.multiple_of(offsets[n], 128)
        out[:, pl.ds(start, width)] = refs[source][:, at : at + width]


def place(pieces, segments, offsets, columns):
    rows = pieces[0].shape[0]
    block = 64 if rows % 64 == 0 else rows
    return pl.pallas_call(
        functools.partial(place_kernel, segments=segments),
        grid_spec=pltpu.PrefetchScalarGridSpec(
            num_scalar_prefetch=1,
            grid=(rows // block,),
            in_specs=[
                pl.BlockSpec((block, piece.shape[1]), lambda i, offsets: (i, 0))
                for piece in pieces
            ],
            out_specs=pl.BlockSpec((block, columns), lambda i, offsets: (i, 0)),
        ),
        out_shape=jax.ShapeDtypeStruct((rows, columns), pieces[0].dtype),
        compiler_params=pltpu.CompilerParams(vmem_limit_bytes=32 << 20),
        cost_estimate=LIGHT,
        name="place",
    )(jnp.stack(offsets).astype(jnp.int32), *pieces)


def cache_kernel(page_of, pages_ref, o_ref):
    slots = o_ref.shape[0]
    first = pl.program_id(0) * slots
    for n in range(slots):
        page = page_of[first + n]
        start = pl.multiple_of(jnp.maximum(page, 0) * PAGE, PAGE)
        rows = pages_ref[pl.ds(start, PAGE), :]
        o_ref[n] = jnp.where(page >= 0, rows, jnp.zeros_like(rows))


def cache_of(pages, page_of):
    rows, width = pages.shape
    count = page_of.shape[0]
    block = 16 if count % 16 == 0 else count
    return pl.pallas_call(
        cache_kernel,
        grid_spec=pltpu.PrefetchScalarGridSpec(
            num_scalar_prefetch=1,
            grid=(count // block,),
            in_specs=[pl.BlockSpec((rows, width), lambda i, page_of: (0, 0))],
            out_specs=pl.BlockSpec((block, PAGE, width), lambda i, page_of: (i, 0, 0)),
        ),
        out_shape=jax.ShapeDtypeStruct((count, PAGE, width), pages.dtype),
        compiler_params=pltpu.CompilerParams(vmem_limit_bytes=32 << 20),
        cost_estimate=LIGHT,
        name="cache",
    )(page_of, pages)


def hop(array, mask):
    count = lax.axis_size("inst")
    return lax.ppermute(array, "inst", [(i, i ^ mask) for i in range(count)])


def swap(array, axis):
    return lax.ppermute(array, axis, [(0, 1), (1, 0)])


def product_kernel(*refs, heights, parts, groups, summed):
    step = pl.program_id(0)
    lefts, refs = refs[: heights * parts], refs[heights * parts :]
    out = refs[-1]
    rows, depth = lefts[0].shape

    def group_of(rights):
        def compute():
            for height in range(heights):
                total = None
                for part in range(parts):
                    span = slice(part * depth, (part + 1) * depth)
                    right = jnp.concatenate([ref[span, :] for ref in rights], axis=1)
                    term = jnp.dot(
                        lefts[height * parts + part][...], right,
                        preferred_element_type=jnp.float32,
                    )
                    total = term if total is None else total + term
                at = slice(height * rows, (height + 1) * rows)
                if summed:
                    total = total + refs[-2][at, :].astype(jnp.float32)
                out[at, :] = total.astype(out.dtype)
        return compute

    first = 0
    for steps, count in groups:
        compute = group_of(refs[:count])
        refs = refs[count:]
        if len(groups) == 1:
            compute()
        else:
            pl.when((step >= first) & (step < first + steps))(compute)
        first += steps


def product(lefts, rights, other=None):
    rows, depth = lefts[0][0].shape
    block = 2 * WIDTH
    operands, specs, groups = [], [], []
    for left in lefts:
        for part in left:
            operands.append(part)
            specs.append(pl.BlockSpec((rows, depth), lambda n: (0, 0)))
    first = 0
    for right in rights:
        if isinstance(right, tuple):
            steps = 1
            for piece in right:
                operands.append(piece)
                specs.append(pl.BlockSpec(piece.shape, lambda n: (0, 0)))
            groups.append((1, len(right)))
        else:
            steps = right.shape[1] // block
            operands.append(right)
            specs.append(
                pl.BlockSpec(
                    (right.shape[0], block),
                    lambda n, first=first, steps=steps: (0, jnp.clip(n - first, 0, steps - 1)),
                )
            )
            groups.append((steps, 1))
        first += steps
    height = rows * len(lefts)
    out_spec = pl.BlockSpec((height, block), lambda n: (0, n))
    if other is not None:
        operands.append(other)
        specs.append(out_spec)
    return pl.pallas_call(
        functools.partial(
            product_kernel, heights=len(lefts), parts=len(lefts[0]), groups=groups,
            summed=other is not None,
        ),
        grid=(first,),
        in_specs=specs,
        out_specs=out_spec,
        out_shape=jax.ShapeDtypeStruct((height, first * block), operands[0].dtype),
        compiler_params=pltpu.CompilerParams(vmem_limit_bytes=56 << 20),
        cost_estimate=LIGHT,
        name="product",
    )(*operands)


def after(array, *earlier):
    return lax.optimization_barrier((array,) + earlier)[0]


def data_pages(tok_rows):
    span = PAGE * OWNERS
    return (tok_rows + REQ_INST * (span - 1)) // span


def packing(lens, residue):
    page_counts = (lens + (PAGE - 1)) // PAGE
    counts = jnp.maximum(page_counts - residue + (OWNERS - 1), 0) // OWNERS
    return counts, jnp.cumsum(counts, axis=-1) - counts


def packed_pages(held, lens, residues, tok_rows):
    limit = data_pages(tok_rows)
    starts = jnp.cumsum(lens) - lens
    residues = jnp.stack(residues)[:, None]
    counts, firsts = packing(lens[None, :], residues)
    slot = jnp.arange(limit + 1, dtype=jnp.int32)
    step = slot[None, :, None] - firsts[:, None, :]
    mine = (step >= 0) & (step < counts[:, None, :])
    offset = (step * OWNERS + residues[:, :, None]) * PAGE
    base = jnp.sum(jnp.where(mine, starts[None, None, :] + offset, 0), axis=2)
    live = jnp.sum(jnp.where(mine, jnp.minimum(lens[None, None, :] - offset, PAGE), 0), axis=2)
    base = jnp.where(slot[None, :] == limit, tok_rows, base)
    live = jnp.where(slot[None, :] == limit, PAGE, live)
    within = jnp.arange(PAGE, dtype=jnp.int32)
    row = jnp.where(
        within[None, None, :] < live[:, :, None], base[:, :, None] + within[None, None, :], -1
    ).reshape(-1)
    chosen = row[:, None] == jnp.arange(held.shape[0], dtype=jnp.int32)[None, :]
    pages = jnp.dot(chosen.astype(held.dtype), held, preferred_element_type=jnp.float32)
    return pages.astype(held.dtype).reshape(residues.shape[0], (limit + 1) * PAGE, held.shape[1])


def slot_pages(lens, placement, page_table, block_of, limit):
    inst_here = lax.axis_index("inst")
    residue = inst_here % OWNERS
    requests = page_table.shape[0]
    slot_count = requests * QUARTERS
    counts, firsts = packing(lens, residue)
    slots = lax.dynamic_index_in_dim(
        page_table.reshape(requests, QUARTERS, OWNERS), residue, axis=2, keepdims=False
    )
    step = jnp.arange(QUARTERS, dtype=jnp.int32)
    valid = (placement == inst_here // OWNERS)[:, None] & (step[None, :] < counts.reshape(-1)[:, None])
    page = (firsts + block_of[:, None] * (limit + 1)).reshape(-1)[:, None] + step[None, :]
    target = jnp.where(valid, slots, slot_count).reshape(-1)
    match = target[None, :] == jnp.arange(slot_count, dtype=jnp.int32)[:, None]
    return jnp.sum(jnp.where(match, page.reshape(-1)[None, :] + 1, 0), axis=1) - 1


def per_device(queries, keys_values, out_weight, lengths, placement, page_table):
    tok_rows = queries.shape[0]
    tp_count = lax.axis_size("tp")
    tp_here = lax.axis_index("tp")
    inst_count = lax.axis_size("inst")
    inst_here = lax.axis_index("inst")
    grp_here = lax.axis_index("grp")
    side_here = inst_here % 2
    next_here = inst_here // NEXT % 2
    local_heads = queries.shape[1] // HD
    first_kv = tp_here * local_heads // (NH // KVH)
    ends = jnp.cumsum(lengths[0])
    depth, own_cols = out_weight.shape
    half_cols = own_cols // 2
    kv_width = keys_values.shape[1] // tp_count

    pairs = half_cols // WIDTH

    gate = ()

    def gated(array):
        return after(array, *gate) if gate else array

    def cut(n, *earlier):
        weight = after(out_weight, *earlier) if earlier else out_weight
        return lax.dynamic_slice(
            weight, (jnp.int32(0), grp_here * half_cols + n * WIDTH), (depth, WIDTH)
        )

    pieces, segments, offsets = [], [], []
    own_columns = [(own_cols, lambda inst: inst * own_cols)]

    def pair_columns(first, last):
        return [
            (
                WIDTH,
                lambda inst, n=n, half=half: (
                    (inst ^ FAR) * own_cols + half * half_cols + n * WIDTH
                ),
            )
            for n in range(first, last)
            for half in (grp_here, 1 - grp_here)
        ]

    def hand_out(mask, share, columns):
        at = 0
        for width, column_of in columns:
            segments.append((len(pieces), at, width))
            offsets.append(column_of(inst_here ^ mask))
            at += width
        pieces.append(hop(share, mask) if mask else share)
        return pieces[-1]

    kv_parts = 2 if local_heads % (2 * (NH // KVH)) == 0 else 1
    blocks = {mask: [] for mask in MASKS}

    def begin_sum(masks, rights):
        lefts = [list(blocks[mask]) for mask in masks]
        lefts[0][0] = gated(lefts[0][0])
        return masks, rights, product([left[:kv_parts] for left in lefts], rights)

    def end_sum(begun, *earlier):
        masks, rights, given = begun
        given = after(given, *earlier) if earlier else given
        if tp_count == 2:
            lefts = [blocks[mask][kv_parts:] for mask in masks]
            total = product(lefts, rights, swap(given, "tp"))
        else:
            total = given
        rows = total.shape[0] // len(masks)
        shares = {mask: total[n * rows : (n + 1) * rows] for n, mask in enumerate(masks)}
        if tp_count != 2:
            for mask in masks:
                shares[mask] = lax.psum_scatter(
                    shares[mask], "tp", scatter_dimension=0, tiled=True
                )
        return total, shares

    def group_sum(masks, rights, *earlier):
        return end_sum(begin_sum(masks, rights), *earlier)

    sliced, along, across = [cut(0)], [], []
    along.append(hop(sliced[0], FAR))
    held = lax.dynamic_slice_in_dim(
        after(keys_values, sliced[0]), tp_here * kv_width, kv_width, 1
    )
    lens_rows = jnp.zeros((PAGE, kv_width), held.dtype)
    lens_rows = lens_rows.at[0, :REQ_INST].set(lengths[0].astype(held.dtype))
    held = jnp.concatenate([held, lens_rows], axis=0)
    held_far = hop(held, FAR)
    chunks = [1 - tp_here, tp_here] if tp_count == 2 else [jnp.int32(0)]
    own = blocks[0]
    ready = held
    for chunk in chunks:
        for part in range(kv_parts):
            ready = attention(
                after(queries, ready), keys_values, ends, first_kv, chunk,
                tok_rows // len(chunks), part, kv_parts,
            )
            own.append(ready)

    def spread(name, arrays, mask):
        sent = [hop(gated(array), mask) for array in arrays]
        blocks[name] += sent
        return tuple(sent)

    moved = spread(NEXT, own[:1], NEXT) + spread(SIDE, own[:2], SIDE)
    for n in range(1, pairs):
        ready = cut(n, ready)
        sliced.append(ready)
    gate = moved + (along[0], held_far, ready)

    def weights():
        n = len(across)
        across.append(swap(gated(along[n]), "grp"))
        if n + 1 < pairs:
            along.append(hop(gated(sliced[n + 1]), FAR))
        return (across[-1], along[-1])

    moved = weights() + spread(NEXT, own[1:2], NEXT) + spread(SIDE, own[2:], SIDE)
    held_far = gated(held_far)
    pages_given, pages_kept = (
        jnp.stack(
            [
                packed_pages(rows, lens, residues, tok_rows)
                for rows, lens in (
                    (held, lengths[0]),
                    (held_far, held_far[tok_rows, :REQ_INST].astype(jnp.int32)),
                )
            ]
        )
        for residues in ([1 - side_here, 3 - side_here], [side_here, 2 + side_here])
    )
    ready, own_shares = group_sum((0,), [out_weight], moved[0])
    gate = moved + (pages_given, pages_kept, ready)

    near = blocks[NEXT]
    moved = weights() + spread(NEXT, own[2:3], NEXT) + spread(NEXT | SIDE, near[:2], SIDE)
    ready, shares = group_sum((SIDE,), [out_weight], moved[0])
    own_shares.update(shares)
    gate = moved + (ready,)

    def pair(n):
        return (along[n], across[n])

    moved = weights() + spread(NEXT, own[3:], NEXT) + spread(NEXT | SIDE, near[2:3], SIDE)
    pages_side = hop(gated(pages_given), SIDE)
    ready, shares = group_sum((0, SIDE), [pair(0), pair(1)], moved[0])
    gate = moved + (pages_side, ready)

    first_columns = own_columns + pair_columns(0, 2)
    moved = weights() + spread(NEXT | SIDE, near[3:], SIDE)
    moved += (
        hand_out(SIDE, gated(jnp.concatenate([own_shares[SIDE], shares[SIDE]], axis=1)), first_columns),
    )
    hand_out(0, own_shares[0], own_columns)
    hand_out(0, shares[0], pair_columns(0, 2))
    pages = gated(jnp.concatenate([pages_kept, pages_side], axis=0))
    pages_next = hop(
        lax.dynamic_index_in_dim(pages, 1 - next_here, axis=1, keepdims=False), NEXT
    )
    pages = lax.dynamic_index_in_dim(pages, next_here, axis=1, keepdims=False)
    ready, shares = group_sum((NEXT,), [out_weight, pair(0), pair(1)], moved[0])
    gate = moved + (pages_next, ready)

    moved = weights() + (hand_out(NEXT, gated(shares[NEXT]), first_columns),)
    begun = begin_sum((NEXT | SIDE,), [out_weight, pair(0), pair(1), pair(2), pair(3)])
    begun_near = begin_sum((SIDE, NEXT, 0), [pair(2), pair(3)])
    far_shares = end_sum(begun, begun_near[2], *moved)[1]
    shares = end_sum(begun_near, *moved)[1]
    pages = jnp.concatenate([pages, gated(pages_next)], axis=0)
    order = [mask ^ far for mask in (0, SIDE) for far in (0, FAR)]
    order = order + [at ^ NEXT for at in order]
    block_of = jnp.asarray([order.index(i) for i in range(inst_count)], jnp.int32)
    block_of = jnp.take(block_of, jnp.arange(inst_count, dtype=jnp.int32) ^ inst_here)
    limit = data_pages(tok_rows)
    lens = jnp.take(pages[:, limit * PAGE, :REQ_INST].astype(jnp.int32), block_of, axis=0)
    page_of = slot_pages(lens, placement, page_table, block_of, limit)
    cache = cache_of(pages.reshape(-1, kv_width), page_of)
    gate = moved + (begun_near[2],)

    moved = weights()
    hand_out(NEXT | SIDE, gated(far_shares[NEXT | SIDE]), own_columns + pair_columns(0, 4))
    for mask in (NEXT, SIDE, 0):
        hand_out(mask, gated(shares[mask]), pair_columns(2, 4))
    masks = (NEXT | SIDE, NEXT, SIDE, 0)
    ready, shares = group_sum(masks, [pair(4)])
    for mask in masks:
        hand_out(mask, shares[mask], pair_columns(4, 5))
    gate = moved + (ready,)
    ready, shares = group_sum(masks, [pair(5)])
    for mask in masks:
        hand_out(mask, shares[mask], pair_columns(5, 6))
    projected = place(pieces, segments, offsets, inst_count * own_cols)
    return (projected, cache)


def solution(mesh):
    return jax.shard_map(
        per_device,
        mesh=mesh,
        in_specs=(
            P(("grp", "inst"), "tp"),
            P(("grp", "inst"), None),
            P("tp", "inst"),
            P(("grp", "inst"), None),
            P("grp"),
            P("grp", None),
        ),
        out_specs=(P(("grp", "inst", "tp"), None), P(("grp", "inst"), None, "tp")),
        check_vma=False,
    )
```

```python
import functools

import jax
import jax.numpy as jnp
from jax import lax
from jax.experimental import pallas as pl
from jax.experimental.pallas import tpu as pltpu
from jax.sharding import PartitionSpec as P

NH = 96
KVH = 8
HD = 128
PAGE = 16
OWNERS = 4
REQ_INST = 4
MAXLEN = 256
QUARTERS = 4
ROWS = 128
LOG2E = 1.4426950408889634

SIDE, NEXT, FAR = 1, 2, 4
MASKS = (0, NEXT, SIDE, NEXT | SIDE)
WIDTH = 128
LIGHT = pl.CostEstimate(flops=0, bytes_accessed=0, transcendentals=0)


def attention_kernel(info, q_ref, k_ref, v_ref, o_ref, *, heads, row_blocks, window):
    for block in range(row_blocks):
        place = info[0] * row_blocks + block
        first = pl.multiple_of(jnp.maximum(place - (window // ROWS - 1), 0) * ROWS, ROWS)
        row = place * ROWS + lax.broadcasted_iota(jnp.int32, (ROWS, window), 0)
        col = first + lax.broadcasted_iota(jnp.int32, (ROWS, window), 1)
        begin = jnp.zeros_like(row)
        for j in range(REQ_INST):
            begin = jnp.where(row >= info[2 + j], info[2 + j], begin)
        bias = jnp.where((col <= row) & (col >= begin), 0.0, -1e30)
        keys = k_ref[pl.ds(first, window), :]
        vals = v_ref[pl.ds(first, window), :]
        vals = jnp.concatenate([vals, jnp.ones_like(vals)], axis=1)
        rows = slice(block * ROWS, (block + 1) * ROWS)
        for head in range(heads):
            cols = slice(head * HD, (head + 1) * HD)
            scores = lax.dot_general(
                q_ref[rows, cols], keys, (((1,), (1,)), ((), ())),
                preferred_element_type=jnp.float32,
            )
            scores = scores * (LOG2E / HD**0.5) + bias
            expo = jnp.exp2(scores - jnp.max(scores, axis=1, keepdims=True))
            mixed = jnp.dot(expo.astype(jnp.bfloat16), vals, preferred_element_type=jnp.float32)
            o_ref[rows, cols] = (mixed[:, :HD] / mixed[:, HD:]).astype(jnp.bfloat16)


def attention(queries, keys_values, ends, first_kv, chunk, chunk_rows, part, parts):
    tok_rows, width = queries.shape
    local_heads = width // HD
    kv_heads = max(1, local_heads // (NH // KVH))
    heads = local_heads // kv_heads
    steps = kv_heads // parts
    window = min(ROWS + MAXLEN, tok_rows)
    first_kv = first_kv + part * steps
    info = jnp.concatenate([jnp.stack([chunk, first_kv]).astype(jnp.int32), ends])
    return pl.pallas_call(
        functools.partial(
            attention_kernel, heads=heads, row_blocks=chunk_rows // ROWS, window=window
        ),
        grid_spec=pltpu.PrefetchScalarGridSpec(
            num_scalar_prefetch=1,
            grid=(steps,),
            in_specs=[
                pl.BlockSpec(
                    (chunk_rows, heads * HD), lambda g, info: (info[0], part * steps + g)
                ),
                pl.BlockSpec((tok_rows, HD), lambda g, info: (0, 2 * (info[1] + g))),
                pl.BlockSpec((tok_rows, HD), lambda g, info: (0, 2 * (info[1] + g) + 1)),
            ],
            out_specs=pl.BlockSpec((chunk_rows, heads * HD), lambda g, info: (0, g)),
        ),
        out_shape=jax.ShapeDtypeStruct((chunk_rows, width // parts), jnp.bfloat16),
        compiler_params=pltpu.CompilerParams(vmem_limit_bytes=32 << 20),
        cost_estimate=LIGHT,
        name="attention",
    )(info, queries, keys_values, keys_values)


def place_kernel(offsets, *refs, segments):
    out = refs[-1]
    for n, (source, at, width) in enumerate(segments):
        start = pl.multiple_of(offsets[n], 128)
        out[:, pl.ds(start, width)] = refs[source][:, at : at + width]


def place(pieces, segments, offsets, columns):
    rows = pieces[0].shape[0]
    block = 64 if rows % 64 == 0 else rows
    return pl.pallas_call(
        functools.partial(place_kernel, segments=segments),
        grid_spec=pltpu.PrefetchScalarGridSpec(
            num_scalar_prefetch=1,
            grid=(rows // block,),
            in_specs=[
                pl.BlockSpec((block, piece.shape[1]), lambda i, offsets: (i, 0))
                for piece in pieces
            ],
            out_specs=pl.BlockSpec((block, columns), lambda i, offsets: (i, 0)),
        ),
        out_shape=jax.ShapeDtypeStruct((rows, columns), pieces[0].dtype),
        compiler_params=pltpu.CompilerParams(vmem_limit_bytes=32 << 20),
        cost_estimate=LIGHT,
        name="place",
    )(jnp.stack(offsets).astype(jnp.int32), *pieces)


def cache_kernel(page_of, pages_ref, o_ref):
    slots = o_ref.shape[0]
    first = pl.program_id(0) * slots
    for n in range(slots):
        page = page_of[first + n]
        start = pl.multiple_of(jnp.maximum(page, 0) * PAGE, PAGE)
        rows = pages_ref[pl.ds(start, PAGE), :]
        o_ref[n] = jnp.where(page >= 0, rows, jnp.zeros_like(rows))


def cache_of(pages, page_of):
    rows, width = pages.shape
    count = page_of.shape[0]
    block = 16 if count % 16 == 0 else count
    return pl.pallas_call(
        cache_kernel,
        grid_spec=pltpu.PrefetchScalarGridSpec(
            num_scalar_prefetch=1,
            grid=(count // block,),
            in_specs=[pl.BlockSpec((rows, width), lambda i, page_of: (0, 0))],
            out_specs=pl.BlockSpec((block, PAGE, width), lambda i, page_of: (i, 0, 0)),
        ),
        out_shape=jax.ShapeDtypeStruct((count, PAGE, width), pages.dtype),
        compiler_params=pltpu.CompilerParams(vmem_limit_bytes=32 << 20),
        cost_estimate=LIGHT,
        name="cache",
    )(page_of, pages)


def hop(array, mask):
    count = lax.axis_size("inst")
    return lax.ppermute(array, "inst", [(i, i ^ mask) for i in range(count)])


def swap(array, axis):
    return lax.ppermute(array, axis, [(0, 1), (1, 0)])


def product_kernel(*refs, heights, parts, groups, summed):
    step = pl.program_id(0)
    lefts, refs = refs[: heights * parts], refs[heights * parts :]
    out = refs[-1]
    rows, depth = lefts[0].shape

    def group_of(rights):
        def compute():
            for height in range(heights):
                total = None
                for part in range(parts):
                    span = slice(part * depth, (part + 1) * depth)
                    right = jnp.concatenate([ref[span, :] for ref in rights], axis=1)
                    term = jnp.dot(
                        lefts[height * parts + part][...], right,
                        preferred_element_type=jnp.float32,
                    )
                    total = term if total is None else total + term
                at = slice(height * rows, (height + 1) * rows)
                if summed:
                    total = total + refs[-2][at, :].astype(jnp.float32)
                out[at, :] = total.astype(out.dtype)
        return compute

    first = 0
    for steps, count in groups:
        compute = group_of(refs[:count])
        refs = refs[count:]
        if len(groups) == 1:
            compute()
        else:
            pl.when((step >= first) & (step < first + steps))(compute)
        first += steps


def product(lefts, rights, other=None):
    rows, depth = lefts[0][0].shape
    block = 4 * WIDTH
    once = pl.Buffered(1)
    operands, specs, groups = [], [], []
    for left in lefts:
        for part in left:
            operands.append(part)
            specs.append(pl.BlockSpec((rows, depth), lambda n: (0, 0), pipeline_mode=once))
    first = 0
    for right in rights:
        if isinstance(right, tuple):
            steps = 1
            for piece in right:
                operands.append(piece)
                specs.append(pl.BlockSpec(piece.shape, lambda n: (0, 0), pipeline_mode=once))
            groups.append((1, len(right)))
        else:
            steps = right.shape[1] // block
            operands.append(right)
            specs.append(
                pl.BlockSpec(
                    (right.shape[0], block),
                    lambda n, first=first, steps=steps: (0, jnp.clip(n - first, 0, steps - 1)),
                )
            )
            groups.append((steps, 1))
        first += steps
    height = rows * len(lefts)
    out_spec = pl.BlockSpec((height, block), lambda n: (0, n))
    if other is not None:
        operands.append(other)
        specs.append(out_spec)
    return pl.pallas_call(
        functools.partial(
            product_kernel, heights=len(lefts), parts=len(lefts[0]), groups=groups,
            summed=other is not None,
        ),
        grid=(first,),
        in_specs=specs,
        out_specs=out_spec,
        out_shape=jax.ShapeDtypeStruct((height, first * block), operands[0].dtype),
        compiler_params=pltpu.CompilerParams(vmem_limit_bytes=56 << 20),
        cost_estimate=LIGHT,
        name="product",
    )(*operands)


def tall_kernel(*refs, heights, pieces, steps, summed):
    lefts, rights = refs[: heights * len(steps)], refs[heights * len(steps) :]
    out, total = refs[-2:]
    step = pl.program_id(0)
    rows = lefts[0].shape[0]

    @pl.when(step == 0)
    def _():
        total[...] = jnp.zeros_like(total)

    def add(part):
        group = rights[part * 2 : part * 2 + 2] if pieces > 1 else rights[:2]
        right = jnp.concatenate([ref[...] for ref in group], axis=1)
        for height in range(heights):
            at = slice(height * rows, (height + 1) * rows)
            total[at, :] += jnp.dot(
                lefts[height * len(steps) + part][...], right, preferred_element_type=jnp.float32
            )

    first = 0
    for part, count in enumerate(steps):
        pl.when((step >= first) & (step < first + count))(functools.partial(add, part))
        first += count

    @pl.when(step == first - 1)
    def _():
        result = total[...]
        if summed:
            result = result + refs[-3][...].astype(jnp.float32)
        out[...] = result.astype(out.dtype)


def tall_product(lefts, rights, other=None):
    rows, depth = lefts[0][0].shape
    parts = len(lefts[0])
    block = depth // 4 if depth % 512 == 0 else depth
    count = depth // block
    steps = (count,) * parts

    def within(part):
        return lambda k: jnp.clip(k - part * count, 0, count - 1)

    operands, specs = [], []
    for left in lefts:
        for part, array in enumerate(left):
            operands.append(array)
            specs.append(
                pl.BlockSpec((rows, block), lambda k, at=within(part): (0, at(k)))
            )
    for part, group in enumerate(rights):
        for array in group:
            operands.append(array)
            at = within(part) if len(rights) > 1 else (lambda k: k)
            specs.append(pl.BlockSpec((block, WIDTH), lambda k, at=at: (at(k), 0)))
    shape = (rows * len(lefts), 2 * WIDTH)
    whole = pl.BlockSpec(shape, lambda k: (0, 0))
    if other is not None:
        operands.append(other)
        specs.append(whole)
    return pl.pallas_call(
        functools.partial(
            tall_kernel, heights=len(lefts), pieces=len(rights), steps=steps,
            summed=other is not None,
        ),
        grid=(count * parts,),
        in_specs=specs,
        out_specs=whole,
        out_shape=jax.ShapeDtypeStruct(shape, operands[0].dtype),
        scratch_shapes=[pltpu.VMEM(shape, jnp.float32)],
        compiler_params=pltpu.CompilerParams(vmem_limit_bytes=56 << 20),
        cost_estimate=LIGHT,
        name="product",
    )(*operands)


def after(array, *earlier):
    return lax.optimization_barrier((array,) + earlier)[0]


def data_pages(tok_rows):
    span = PAGE * OWNERS
    return (tok_rows + REQ_INST * (span - 1)) // span


def packing(lens, residue):
    page_counts = (lens + (PAGE - 1)) // PAGE
    counts = jnp.maximum(page_counts - residue + (OWNERS - 1), 0) // OWNERS
    return counts, jnp.cumsum(counts, axis=-1) - counts


def packed_pages(held, lens, residues, tok_rows):
    limit = data_pages(tok_rows)
    starts = jnp.cumsum(lens) - lens
    residues = jnp.stack(residues)[:, None]
    counts, firsts = packing(lens[None, :], residues)
    slot = jnp.arange(limit + 1, dtype=jnp.int32)
    step = slot[None, :, None] - firsts[:, None, :]
    mine = (step >= 0) & (step < counts[:, None, :])
    offset = (step * OWNERS + residues[:, :, None]) * PAGE
    base = jnp.sum(jnp.where(mine, starts[None, None, :] + offset, 0), axis=2)
    live = jnp.sum(jnp.where(mine, jnp.minimum(lens[None, None, :] - offset, PAGE), 0), axis=2)
    base = jnp.where(slot[None, :] == limit, tok_rows, base)
    live = jnp.where(slot[None, :] == limit, PAGE, live)
    within = jnp.arange(PAGE, dtype=jnp.int32)
    row = jnp.where(
        within[None, None, :] < live[:, :, None], base[:, :, None] + within[None, None, :], -1
    ).reshape(-1)
    chosen = row[:, None] == jnp.arange(held.shape[0], dtype=jnp.int32)[None, :]
    pages = jnp.dot(chosen.astype(held.dtype), held, preferred_element_type=jnp.float32)
    return pages.astype(held.dtype).reshape(residues.shape[0], (limit + 1) * PAGE, held.shape[1])


def slot_pages(lens, placement, page_table, block_of, limit):
    inst_here = lax.axis_index("inst")
    residue = inst_here % OWNERS
    requests = page_table.shape[0]
    slot_count = requests * QUARTERS
    counts, firsts = packing(lens, residue)
    slots = lax.dynamic_index_in_dim(
        page_table.reshape(requests, QUARTERS, OWNERS), residue, axis=2, keepdims=False
    )
    step = jnp.arange(QUARTERS, dtype=jnp.int32)
    valid = (placement == inst_here // OWNERS)[:, None] & (step[None, :] < counts.reshape(-1)[:, None])
    page = (firsts + block_of[:, None] * (limit + 1)).reshape(-1)[:, None] + step[None, :]
    target = jnp.where(valid, slots, slot_count).reshape(-1)
    match = target[None, :] == jnp.arange(slot_count, dtype=jnp.int32)[:, None]
    return jnp.sum(jnp.where(match, page.reshape(-1)[None, :] + 1, 0), axis=1) - 1


def per_device(queries, keys_values, out_weight, lengths, placement, page_table):
    tok_rows = queries.shape[0]
    tp_count = lax.axis_size("tp")
    tp_here = lax.axis_index("tp")
    inst_count = lax.axis_size("inst")
    inst_here = lax.axis_index("inst")
    grp_here = lax.axis_index("grp")
    side_here = inst_here % 2
    next_here = inst_here // NEXT % 2
    local_heads = queries.shape[1] // HD
    first_kv = tp_here * local_heads // (NH // KVH)
    ends = jnp.cumsum(lengths[0])
    depth, own_cols = out_weight.shape
    half_cols = own_cols // 2
    kv_width = keys_values.shape[1] // tp_count

    pairs = half_cols // WIDTH

    gate = ()

    def gated(array):
        return after(array, *gate) if gate else array

    def cut(n, *earlier):
        weight = after(out_weight, *earlier) if earlier else out_weight
        return lax.dynamic_slice(
            weight, (jnp.int32(0), grp_here * half_cols + n * WIDTH), (depth, WIDTH)
        )

    pieces, segments, offsets = [], [], []
    own_columns = [(own_cols, lambda inst: inst * own_cols)]

    def pair_columns(first, last):
        return [
            (
                WIDTH,
                lambda inst, n=n, half=half: (
                    (inst ^ FAR) * own_cols + half * half_cols + n * WIDTH
                ),
            )
            for n in range(first, last)
            for half in (grp_here, 1 - grp_here)
        ]

    def hand_out(mask, share, columns):
        at = 0
        for width, column_of in columns:
            segments.append((len(pieces), at, width))
            offsets.append(column_of(inst_here ^ mask))
            at += width
        pieces.append(hop(share, mask) if mask else share)
        return pieces[-1]

    kv_parts = 2 if local_heads % (2 * (NH // KVH)) == 0 else 1
    blocks = {mask: [] for mask in MASKS}

    def begin_sum(masks, rights, multiply=product):
        lefts = [list(blocks[mask]) for mask in masks]
        lefts[0][0] = gated(lefts[0][0])
        return masks, rights, multiply([left[:kv_parts] for left in lefts], rights), multiply

    def end_sum(begun, *earlier):
        masks, rights, given, multiply = begun
        given = after(given, *earlier) if earlier else given
        if tp_count == 2:
            lefts = [blocks[mask][kv_parts:] for mask in masks]
            total = multiply(lefts, rights, swap(given, "tp"))
        else:
            total = given
        rows = total.shape[0] // len(masks)
        shares = {mask: total[n * rows : (n + 1) * rows] for n, mask in enumerate(masks)}
        if tp_count != 2:
            for mask in masks:
                shares[mask] = lax.psum_scatter(
                    shares[mask], "tp", scatter_dimension=0, tiled=True
                )
        return total, shares

    def group_sum(masks, rights, *earlier, multiply=product):
        return end_sum(begin_sum(masks, rights, multiply), *earlier)

    sliced, along, across = [cut(0)], [], []
    along.append(hop(sliced[0], FAR))
    held = lax.dynamic_slice_in_dim(
        after(keys_values, sliced[0]), tp_here * kv_width, kv_width, 1
    )
    lens_rows = jnp.zeros((PAGE, kv_width), held.dtype)
    lens_rows = lens_rows.at[0, :REQ_INST].set(lengths[0].astype(held.dtype))
    held = jnp.concatenate([held, lens_rows], axis=0)
    held_far = hop(held, FAR)
    chunks = [1 - tp_here, tp_here] if tp_count == 2 else [jnp.int32(0)]
    own = blocks[0]
    ready = held
    for chunk in chunks:
        for part in range(kv_parts):
            ready = attention(
                after(queries, ready), keys_values, ends, first_kv, chunk,
                tok_rows // len(chunks), part, kv_parts,
            )
            own.append(ready)

    def spread(name, arrays, mask):
        sent = [hop(gated(array), mask) for array in arrays]
        blocks[name] += sent
        return tuple(sent)

    moved = spread(NEXT, own[:1], NEXT) + spread(SIDE, own[:2], SIDE)
    for n in range(1, pairs):
        ready = cut(n, ready)
        sliced.append(ready)
    gate = moved + (along[0], held_far, ready)

    def weights():
        n = len(across)
        across.append(swap(gated(along[n]), "grp"))
        if n + 1 < pairs:
            along.append(hop(gated(sliced[n + 1]), FAR))
        return (across[-1], along[-1])

    moved = weights() + spread(NEXT, own[1:2], NEXT) + spread(SIDE, own[2:], SIDE)
    held_far = gated(held_far)
    pages_given, pages_kept = (
        jnp.stack(
            [
                packed_pages(rows, lens, residues, tok_rows)
                for rows, lens in (
                    (held, lengths[0]),
                    (held_far, held_far[tok_rows, :REQ_INST].astype(jnp.int32)),
                )
            ]
        )
        for residues in ([1 - side_here, 3 - side_here], [side_here, 2 + side_here])
    )
    ready, own_shares = group_sum((0,), [out_weight], moved[0])
    gate = moved + (pages_given, pages_kept, ready)

    near = blocks[NEXT]
    moved = weights() + spread(NEXT, own[2:3], NEXT) + spread(NEXT | SIDE, near[:2], SIDE)
    ready, shares = group_sum((SIDE,), [out_weight], moved[0])
    own_shares.update(shares)
    gate = moved + (ready,)

    def two_pairs(n):
        return (along[n], across[n], along[n + 1], across[n + 1])

    moved = weights() + spread(NEXT, own[3:], NEXT) + spread(NEXT | SIDE, near[2:3], SIDE)
    pages_side = hop(gated(pages_given), SIDE)
    ready, shares = group_sum((0, SIDE), [two_pairs(0)], moved[0])
    gate = moved + (pages_side, ready)

    first_columns = own_columns + pair_columns(0, 2)
    moved = weights() + spread(NEXT | SIDE, near[3:], SIDE)
    moved += (
        hand_out(SIDE, gated(jnp.concatenate([own_shares[SIDE], shares[SIDE]], axis=1)), first_columns),
    )
    hand_out(0, own_shares[0], own_columns)
    hand_out(0, shares[0], pair_columns(0, 2))
    pages = gated(jnp.concatenate([pages_kept, pages_side], axis=0))
    pages_next = hop(
        lax.dynamic_index_in_dim(pages, 1 - next_here, axis=1, keepdims=False), NEXT
    )
    pages = lax.dynamic_index_in_dim(pages, next_here, axis=1, keepdims=False)
    ready, shares = group_sum((NEXT,), [out_weight, two_pairs(0)], moved[0])
    gate = moved + (pages_next, ready)

    last_piece = [
        sliced[pairs - 1][part * depth // kv_parts : (part + 1) * depth // kv_parts]
        for part in range(kv_parts)
    ]
    across.append(swap(gated(along[-1]), "grp"))
    last_along = [hop(gated(last_piece[0]), FAR)]
    moved = (across[-1], last_along[0], hand_out(NEXT, gated(shares[NEXT]), first_columns))
    begun = begin_sum((NEXT | SIDE,), [out_weight, two_pairs(0), two_pairs(2)])
    begun_near = begin_sum((SIDE, NEXT, 0), [two_pairs(2)])
    pages = jnp.concatenate([pages, gated(pages_next)], axis=0)
    order = [mask ^ far for mask in (0, SIDE) for far in (0, FAR)]
    order = order + [at ^ NEXT for at in order]
    block_of = jnp.asarray([order.index(i) for i in range(inst_count)], jnp.int32)
    block_of = jnp.take(block_of, jnp.arange(inst_count, dtype=jnp.int32) ^ inst_here)
    limit = data_pages(tok_rows)
    lens = jnp.take(pages[:, limit * PAGE, :REQ_INST].astype(jnp.int32), block_of, axis=0)
    page_of = slot_pages(lens, placement, page_table, block_of, limit)
    cache = cache_of(pages.reshape(-1, kv_width), page_of)
    ready, far_shares = end_sum(begun, begun_near[2], last_along[0])
    near_ready, shares = end_sum(begun_near, begun[2], last_along[0])
    last_across = []
    for part in range(1, kv_parts):
        last_along.append(hop(after(last_piece[part], last_along[-1], across[-1]), FAR))
        last_across.append(swap(after(last_along[part - 1], across[-1]), "grp"))
    gate = moved + (cache, ready, near_ready) + tuple(last_along) + tuple(last_across)

    last_across.append(swap(gated(last_along[-1]), "grp"))
    moved = (last_across[-1],)
    hand_out(NEXT | SIDE, gated(far_shares[NEXT | SIDE]), own_columns + pair_columns(0, 4))
    for mask in (NEXT, SIDE, 0):
        moved += (hand_out(mask, gated(shares[mask]), pair_columns(2, 4)),)
    masks = (NEXT | SIDE, NEXT, SIDE, 0)
    ready, shares = group_sum(masks, [(along[4], across[4])], multiply=tall_product)
    for mask in masks:
        hand_out(mask, shares[mask], pair_columns(4, 5))
    gate = moved + (ready,)
    ready, shares = group_sum(
        masks, list(zip(last_along, last_across)), multiply=tall_product
    )
    for mask in masks:
        hand_out(mask, shares[mask], pair_columns(5, 6))
    projected = place(pieces, segments, offsets, inst_count * own_cols)
    return (projected, cache)


def solution(mesh):
    return jax.shard_map(
        per_device,
        mesh=mesh,
        in_specs=(
            P(("grp", "inst"), "tp"),
            P(("grp", "inst"), None),
            P("tp", "inst"),
            P(("grp", "inst"), None),
            P("grp"),
            P("grp", None),
        ),
        out_specs=(P(("grp", "inst", "tp"), None), P(("grp", "inst"), None, "tp")),
        check_vma=False,
    )
```

```python
import functools

import jax
import jax.numpy as jnp
from jax import lax
from jax.experimental import pallas as pl
from jax.experimental.pallas import tpu as pltpu
from jax.sharding import PartitionSpec as P

NH = 96
KVH = 8
HD = 128
PAGE = 16
OWNERS = 4
REQ_INST = 4
MAXLEN = 256
QUARTERS = 4
ROWS = 128
LOG2E = 1.4426950408889634

SIDE, NEXT, FAR = 1, 2, 4
MASKS = (0, NEXT, SIDE, NEXT | SIDE)
WIDTH = 128
LIGHT = pl.CostEstimate(flops=0, bytes_accessed=0, transcendentals=0)


def attention_kernel(info, q_ref, k_ref, v_ref, o_ref, *, heads, row_blocks, window):
    for block in range(row_blocks):
        place = info[0] * row_blocks + block
        first = pl.multiple_of(jnp.maximum(place - (window // ROWS - 1), 0) * ROWS, ROWS)
        row = place * ROWS + lax.broadcasted_iota(jnp.int32, (ROWS, window), 0)
        col = first + lax.broadcasted_iota(jnp.int32, (ROWS, window), 1)
        begin = jnp.zeros_like(row)
        for j in range(REQ_INST):
            begin = jnp.where(row >= info[2 + j], info[2 + j], begin)
        bias = jnp.where((col <= row) & (col >= begin), 0.0, -1e30)
        keys = k_ref[pl.ds(first, window), :]
        vals = v_ref[pl.ds(first, window), :]
        vals = jnp.concatenate([vals, jnp.ones_like(vals)], axis=1)
        rows = slice(block * ROWS, (block + 1) * ROWS)
        for head in range(heads):
            cols = slice(head * HD, (head + 1) * HD)
            scores = lax.dot_general(
                q_ref[rows, cols], keys, (((1,), (1,)), ((), ())),
                preferred_element_type=jnp.float32,
            )
            scores = scores * (LOG2E / HD**0.5) + bias
            expo = jnp.exp2(scores - jnp.max(scores, axis=1, keepdims=True))
            mixed = jnp.dot(expo.astype(jnp.bfloat16), vals, preferred_element_type=jnp.float32)
            o_ref[rows, cols] = (mixed[:, :HD] / mixed[:, HD:]).astype(jnp.bfloat16)


def attention(queries, keys_values, ends, first_kv, chunk, chunk_rows, part, parts):
    tok_rows, width = queries.shape
    local_heads = width // HD
    kv_heads = max(1, local_heads // (NH // KVH))
    heads = local_heads // kv_heads
    steps = kv_heads // parts
    window = min(ROWS + MAXLEN, tok_rows)
    first_kv = first_kv + part * steps
    info = jnp.concatenate([jnp.stack([chunk, first_kv]).astype(jnp.int32), ends])
    return pl.pallas_call(
        functools.partial(
            attention_kernel, heads=heads, row_blocks=chunk_rows // ROWS, window=window
        ),
        grid_spec=pltpu.PrefetchScalarGridSpec(
            num_scalar_prefetch=1,
            grid=(steps,),
            in_specs=[
                pl.BlockSpec(
                    (chunk_rows, heads * HD), lambda g, info: (info[0], part * steps + g)
                ),
                pl.BlockSpec((tok_rows, HD), lambda g, info: (0, 2 * (info[1] + g))),
                pl.BlockSpec((tok_rows, HD), lambda g, info: (0, 2 * (info[1] + g) + 1)),
            ],
            out_specs=pl.BlockSpec((chunk_rows, heads * HD), lambda g, info: (0, g)),
        ),
        out_shape=jax.ShapeDtypeStruct((chunk_rows, width // parts), jnp.bfloat16),
        compiler_params=pltpu.CompilerParams(vmem_limit_bytes=32 << 20),
        cost_estimate=LIGHT,
        name="attention",
    )(info, queries, keys_values, keys_values)


def place_kernel(offsets, *refs, segments):
    out = refs[-1]
    for n, (source, at, width) in enumerate(segments):
        start = pl.multiple_of(offsets[n], 128)
        out[:, pl.ds(start, width)] = refs[source][:, at : at + width]


def place(pieces, segments, offsets, columns):
    rows = pieces[0].shape[0]
    block = 64 if rows % 64 == 0 else rows
    return pl.pallas_call(
        functools.partial(place_kernel, segments=segments),
        grid_spec=pltpu.PrefetchScalarGridSpec(
            num_scalar_prefetch=1,
            grid=(rows // block,),
            in_specs=[
                pl.BlockSpec((block, piece.shape[1]), lambda i, offsets: (i, 0))
                for piece in pieces
            ],
            out_specs=pl.BlockSpec((block, columns), lambda i, offsets: (i, 0)),
        ),
        out_shape=jax.ShapeDtypeStruct((rows, columns), pieces[0].dtype),
        compiler_params=pltpu.CompilerParams(vmem_limit_bytes=32 << 20),
        cost_estimate=LIGHT,
        name="place",
    )(jnp.stack(offsets).astype(jnp.int32), *pieces)


def cache_kernel(page_of, pages_ref, o_ref):
    slots = o_ref.shape[0]
    first = pl.program_id(0) * slots
    for n in range(slots):
        page = page_of[first + n]
        start = pl.multiple_of(jnp.maximum(page, 0) * PAGE, PAGE)
        rows = pages_ref[pl.ds(start, PAGE), :]
        o_ref[n] = jnp.where(page >= 0, rows, jnp.zeros_like(rows))


def cache_of(pages, page_of):
    rows, width = pages.shape
    count = page_of.shape[0]
    block = 16 if count % 16 == 0 else count
    return pl.pallas_call(
        cache_kernel,
        grid_spec=pltpu.PrefetchScalarGridSpec(
            num_scalar_prefetch=1,
            grid=(count // block,),
            in_specs=[pl.BlockSpec((rows, width), lambda i, page_of: (0, 0))],
            out_specs=pl.BlockSpec((block, PAGE, width), lambda i, page_of: (i, 0, 0)),
        ),
        out_shape=jax.ShapeDtypeStruct((count, PAGE, width), pages.dtype),
        compiler_params=pltpu.CompilerParams(vmem_limit_bytes=32 << 20),
        cost_estimate=LIGHT,
        name="cache",
    )(page_of, pages)


def hop(array, mask):
    count = lax.axis_size("inst")
    return lax.ppermute(array, "inst", [(i, i ^ mask) for i in range(count)])


def swap(array, axis):
    return lax.ppermute(array, axis, [(0, 1), (1, 0)])


def product_kernel(*refs, heights, parts, groups, narrow, others):
    step = pl.program_id(0)
    held, sems = refs[-2 - narrow : -2], refs[-1]
    lefts = refs[-2]
    count = heights * parts
    left_refs, refs = refs[:count], refs[count : -2 - narrow]
    sources, wide, at = [], [], 0
    for steps, size in groups:
        wide.append(refs[at] if size == 0 else None)
        if size:
            sources.extend(refs[at : at + size])
        at += max(size, 1)
    out, summands = refs[at + others], refs[at : at + others]
    rows, depth = left_refs[0].shape
    copies = [
        pltpu.make_async_copy(ref, lefts.at[n], sems.at[n]) for n, ref in enumerate(left_refs)
    ]
    narrow_copies = [
        pltpu.make_async_copy(ref, held[n], sems.at[count + n]) for n, ref in enumerate(sources)
    ]

    def start():
        order = copies + narrow_copies if groups[0][1] == 0 else narrow_copies + copies
        for copy in order:
            copy.start()

    def compute(right_of, arrived, first):
        for copy in arrived:
            copy.wait()
        for height in range(heights):
            total = None
            for part in range(parts):
                if first == 0:
                    wait = copies[height * parts + part].wait
                    if groups[0][0] == 1:
                        wait()
                    else:
                        pl.when(step == 0)(wait)
                term = jnp.dot(
                    lefts[height * parts + part], right_of(part),
                    preferred_element_type=jnp.float32,
                )
                total = term if total is None else total + term
            at = slice(height * rows, (height + 1) * rows)
            for other in summands:
                total = total + other[at, :].astype(jnp.float32)
            out[at, :] = total.astype(out.dtype)

    def within(ref, part):
        return ref[part * depth : (part + 1) * depth, :]

    first, used = 0, 0
    if sum(steps for steps, _ in groups) == 1:
        start()
    else:
        pl.when(step == 0)(start)
    for (steps, size), ref in zip(groups, wide):
        if size == 0:
            arrived = []
            right_of = lambda part, ref=ref: within(ref, part)
        else:
            arrived = narrow_copies[used : used + size]
            mine = held[used : used + size]
            right_of = lambda part, mine=mine: jnp.concatenate(
                [within(ref, part) for ref in mine], axis=1
            )
            used += size
        body = functools.partial(compute, right_of, arrived, first)
        if len(groups) == 1:
            body()
        else:
            pl.when((step >= first) & (step < first + steps))(body)
        first += steps


def product(lefts, rights, *others, dtype=jnp.bfloat16):
    rows, depth = lefts[0][0].shape
    sizes = [len(right) * WIDTH for right in rights if isinstance(right, tuple)]
    block = sizes[0] if sizes else 4 * WIDTH
    operands = [part for left in lefts for part in left]
    anywhere = pl.BlockSpec(memory_space=pl.ANY)
    specs = [anywhere] * len(operands)
    count, groups, held = len(operands), [], []
    first = 0
    for right in rights:
        if isinstance(right, tuple):
            steps = 1
            operands += right
            specs += [anywhere] * len(right)
            held += [pltpu.VMEM(piece.shape, piece.dtype) for piece in right]
            groups.append((1, len(right)))
        else:
            steps = right.shape[1] // block
            operands.append(right)
            specs.append(
                pl.BlockSpec(
                    (right.shape[0], block),
                    lambda n, first=first, steps=steps: (0, jnp.clip(n - first, 0, steps - 1)),
                )
            )
            groups.append((steps, 0))
        first += steps
    height = rows * len(lefts)
    out_spec = pl.BlockSpec((height, block), lambda n: (0, n))
    operands += others
    specs += [out_spec] * len(others)
    return pl.pallas_call(
        functools.partial(
            product_kernel, heights=len(lefts), parts=len(lefts[0]), groups=groups,
            narrow=len(held), others=len(others),
        ),
        grid=(first,),
        in_specs=specs,
        out_specs=out_spec,
        out_shape=jax.ShapeDtypeStruct((height, first * block), dtype),
        scratch_shapes=held + [
            pltpu.VMEM((count, rows, depth), operands[0].dtype),
            pltpu.SemaphoreType.DMA((count + len(held),)),
        ],
        compiler_params=pltpu.CompilerParams(vmem_limit_bytes=56 << 20),
        cost_estimate=LIGHT,
        name="product",
    )(*operands)


def after(array, *earlier):
    return lax.optimization_barrier((array,) + earlier)[0]


def data_pages(tok_rows):
    span = PAGE * OWNERS
    return (tok_rows + REQ_INST * (span - 1)) // span


def packing(lens, residue):
    page_counts = (lens + (PAGE - 1)) // PAGE
    counts = jnp.maximum(page_counts - residue + (OWNERS - 1), 0) // OWNERS
    return counts, jnp.cumsum(counts, axis=-1) - counts


def packed_pages(held, lens, residues, tok_rows):
    limit = data_pages(tok_rows)
    starts = jnp.cumsum(lens) - lens
    residues = jnp.stack(residues)[:, None]
    counts, firsts = packing(lens[None, :], residues)
    slot = jnp.arange(limit + 1, dtype=jnp.int32)
    step = slot[None, :, None] - firsts[:, None, :]
    mine = (step >= 0) & (step < counts[:, None, :])
    offset = (step * OWNERS + residues[:, :, None]) * PAGE
    base = jnp.sum(jnp.where(mine, starts[None, None, :] + offset, 0), axis=2)
    live = jnp.sum(jnp.where(mine, jnp.minimum(lens[None, None, :] - offset, PAGE), 0), axis=2)
    base = jnp.where(slot[None, :] == limit, tok_rows, base)
    live = jnp.where(slot[None, :] == limit, PAGE, live)
    within = jnp.arange(PAGE, dtype=jnp.int32)
    row = jnp.where(
        within[None, None, :] < live[:, :, None], base[:, :, None] + within[None, None, :], -1
    ).reshape(-1)
    chosen = row[:, None] == jnp.arange(held.shape[0], dtype=jnp.int32)[None, :]
    pages = jnp.dot(chosen.astype(held.dtype), held, preferred_element_type=jnp.float32)
    return pages.astype(held.dtype).reshape(residues.shape[0], (limit + 1) * PAGE, held.shape[1])


def slot_pages(lens, placement, page_table, block_of, limit):
    inst_here = lax.axis_index("inst")
    residue = inst_here % OWNERS
    requests = page_table.shape[0]
    slot_count = requests * QUARTERS
    counts, firsts = packing(lens, residue)
    slots = lax.dynamic_index_in_dim(
        page_table.reshape(requests, QUARTERS, OWNERS), residue, axis=2, keepdims=False
    )
    step = jnp.arange(QUARTERS, dtype=jnp.int32)
    valid = (placement == inst_here // OWNERS)[:, None] & (step[None, :] < counts.reshape(-1)[:, None])
    page = (firsts + block_of[:, None] * (limit + 1)).reshape(-1)[:, None] + step[None, :]
    target = jnp.where(valid, slots, slot_count).reshape(-1)
    match = target[None, :] == jnp.arange(slot_count, dtype=jnp.int32)[:, None]
    return jnp.sum(jnp.where(match, page.reshape(-1)[None, :] + 1, 0), axis=1) - 1


def per_device(queries, keys_values, out_weight, lengths, placement, page_table):
    tok_rows = queries.shape[0]
    tp_count = lax.axis_size("tp")
    tp_here = lax.axis_index("tp")
    inst_count = lax.axis_size("inst")
    inst_here = lax.axis_index("inst")
    grp_here = lax.axis_index("grp")
    side_here = inst_here % 2
    next_here = inst_here // NEXT % 2
    local_heads = queries.shape[1] // HD
    first_kv = tp_here * local_heads // (NH // KVH)
    ends = jnp.cumsum(lengths[0])
    depth, own_cols = out_weight.shape
    half_cols = own_cols // 2
    kv_width = keys_values.shape[1] // tp_count

    pairs = half_cols // WIDTH

    gate = ()

    def gated(array):
        return after(array, *gate) if gate else array

    def cut(n, *earlier):
        weight = after(out_weight, *earlier) if earlier else out_weight
        return lax.dynamic_slice(
            weight, (jnp.int32(0), grp_here * half_cols + n * WIDTH), (depth, WIDTH)
        )

    pieces, segments, offsets = [], [], []
    own_columns = [(own_cols, lambda inst: inst * own_cols)]

    def pair_columns(first, last):
        return [
            (
                WIDTH,
                lambda inst, n=n, half=half: (
                    (inst ^ FAR) * own_cols + half * half_cols + n * WIDTH
                ),
            )
            for n in range(first, last)
            for half in (grp_here, 1 - grp_here)
        ]

    def hand_out(mask, share, columns):
        at = 0
        for width, column_of in columns:
            segments.append((len(pieces), at, width))
            offsets.append(column_of(inst_here ^ mask))
            at += width
        pieces.append(hop(share, mask) if mask else share)
        return pieces[-1]

    kv_parts = 2 if local_heads % (2 * (NH // KVH)) == 0 else 1
    blocks = {mask: [] for mask in MASKS}

    def begin_sum(masks, rights):
        lefts = [list(blocks[mask]) for mask in masks]
        lefts[0][0] = gated(lefts[0][0])
        return masks, rights, product([left[:kv_parts] for left in lefts], rights)

    def shares_of(total, masks):
        rows = total.shape[0] // len(masks)
        shares = {mask: total[n * rows : (n + 1) * rows] for n, mask in enumerate(masks)}
        if tp_count != 2:
            for mask in masks:
                shares[mask] = lax.psum_scatter(
                    shares[mask], "tp", scatter_dimension=0, tiled=True
                )
        return total, shares

    def end_sum(begun, *earlier):
        masks, rights, given = begun
        total = after(given, *earlier) if earlier else given
        if tp_count == 2:
            lefts = [blocks[mask][kv_parts:] for mask in masks]
            total = product(lefts, rights, swap(total, "tp"))
        return shares_of(total, masks)

    def group_sum(masks, rights, *earlier):
        return end_sum(begin_sum(masks, rights), *earlier)

    sliced, along, across = [cut(0)], [], []
    along.append(hop(sliced[0], FAR))
    held = lax.dynamic_slice_in_dim(
        after(keys_values, sliced[0]), tp_here * kv_width, kv_width, 1
    )
    lens_rows = jnp.zeros((PAGE, kv_width), held.dtype)
    lens_rows = lens_rows.at[0, :REQ_INST].set(lengths[0].astype(held.dtype))
    held = jnp.concatenate([held, lens_rows], axis=0)
    held_far = hop(held, FAR)
    chunks = [1 - tp_here, tp_here] if tp_count == 2 else [jnp.int32(0)]
    own = blocks[0]
    ready = held
    for chunk in chunks:
        for part in range(kv_parts):
            ready = attention(
                after(queries, ready), keys_values, ends, first_kv, chunk,
                tok_rows // len(chunks), part, kv_parts,
            )
            own.append(ready)

    def spread(name, arrays, mask):
        sent = [hop(gated(array), mask) for array in arrays]
        blocks[name] += sent
        return tuple(sent)

    moved = spread(NEXT, own[:1], NEXT) + spread(SIDE, own[:2], SIDE)
    for n in range(1, pairs):
        ready = cut(n, ready)
        sliced.append(ready)
    gate = moved + (along[0], held_far, ready)

    def weights():
        n = len(across)
        across.append(swap(gated(along[n]), "grp"))
        if n + 1 < pairs:
            along.append(hop(gated(sliced[n + 1]), FAR))
        return (across[-1], along[-1])

    moved = weights() + spread(NEXT, own[1:2], NEXT) + spread(SIDE, own[2:], SIDE)
    held_far = gated(held_far)
    pages_given, pages_kept = (
        jnp.stack(
            [
                packed_pages(rows, lens, residues, tok_rows)
                for rows, lens in (
                    (held, lengths[0]),
                    (held_far, held_far[tok_rows, :REQ_INST].astype(jnp.int32)),
                )
            ]
        )
        for residues in ([1 - side_here, 3 - side_here], [side_here, 2 + side_here])
    )
    ready, own_shares = group_sum((0,), [out_weight], moved[0])
    gate = moved + (pages_given, pages_kept, ready)

    near = blocks[NEXT]
    moved = weights() + spread(NEXT, own[2:3], NEXT) + spread(NEXT | SIDE, near[:2], SIDE)
    ready, shares = group_sum((SIDE,), [out_weight], moved[0])
    own_shares.update(shares)
    gate = moved + (ready,)

    def two_pairs(n):
        return (along[n], across[n], along[n + 1], across[n + 1])

    moved = weights() + spread(NEXT, own[3:], NEXT) + spread(NEXT | SIDE, near[2:3], SIDE)
    pages_side = hop(gated(pages_given), SIDE)
    ready, shares = group_sum((0, SIDE), [two_pairs(0)], moved[0])
    gate = moved + (pages_side, ready)

    first_columns = own_columns + pair_columns(0, 2)
    moved = weights() + spread(NEXT | SIDE, near[3:], SIDE)
    moved += (
        hand_out(SIDE, gated(jnp.concatenate([own_shares[SIDE], shares[SIDE]], axis=1)), first_columns),
    )
    hand_out(0, own_shares[0], own_columns)
    hand_out(0, shares[0], pair_columns(0, 2))
    pages = gated(jnp.concatenate([pages_kept, pages_side], axis=0))
    pages_next = hop(
        lax.dynamic_index_in_dim(pages, 1 - next_here, axis=1, keepdims=False), NEXT
    )
    pages = lax.dynamic_index_in_dim(pages, next_here, axis=1, keepdims=False)
    ready, shares = group_sum((NEXT,), [out_weight, two_pairs(0)], moved[0])
    begun_near = begin_sum((SIDE, NEXT, 0), [tuple(after(two_pairs(2), ready))])
    gate = moved + (pages_next, begun_near[2])

    last_piece = [
        sliced[pairs - 1][part * depth // kv_parts : (part + 1) * depth // kv_parts]
        for part in range(kv_parts)
    ]
    across.append(swap(gated(along[-1]), "grp"))
    last_along = [hop(gated(last_piece[0]), FAR)]
    moved = (across[-1], last_along[0], hand_out(NEXT, gated(shares[NEXT]), first_columns))
    begun = begin_sum((NEXT | SIDE,), [out_weight, two_pairs(0), two_pairs(2)])
    pages = jnp.concatenate([pages, gated(pages_next)], axis=0)
    order = [mask ^ far for mask in (0, SIDE) for far in (0, FAR)]
    order = order + [at ^ NEXT for at in order]
    block_of = jnp.asarray([order.index(i) for i in range(inst_count)], jnp.int32)
    block_of = jnp.take(block_of, jnp.arange(inst_count, dtype=jnp.int32) ^ inst_here)
    limit = data_pages(tok_rows)
    lens = jnp.take(pages[:, limit * PAGE, :REQ_INST].astype(jnp.int32), block_of, axis=0)
    page_of = slot_pages(lens, placement, page_table, block_of, limit)
    cache = cache_of(pages.reshape(-1, kv_width), page_of)
    near_ready, shares = end_sum(begun_near, begun[2], last_along[0])
    moved += tuple(
        hand_out(mask, shares[mask], pair_columns(2, 4)) for mask in (NEXT, SIDE, 0)
    )
    ready, far_shares = end_sum(begun, begun[2], last_along[0])
    last_across = []
    for part in range(1, kv_parts):
        last_along.append(hop(after(last_piece[part], last_along[-1], across[-1]), FAR))
        last_across.append(swap(after(last_along[part - 1], across[-1]), "grp"))
    gate = moved + (cache, ready, near_ready) + tuple(last_along) + tuple(last_across)

    last_across.append(swap(gated(last_along[-1]), "grp"))
    hand_out(NEXT | SIDE, gated(far_shares[NEXT | SIDE]), own_columns + pair_columns(0, 4))
    masks = (NEXT | SIDE, NEXT, SIDE, 0)
    ready = gate

    def last_product(chunk, parts, rights, *others, dtype=jnp.float32):
        lefts = [[blocks[mask][chunk * kv_parts + part] for part in parts] for mask in masks]
        return product(lefts, [after(rights, *ready)], *others, dtype=dtype)

    def begin(chunk):
        nonlocal ready
        fourth = last_product(
            chunk, range(kv_parts), (along[4], across[4]),
            dtype=jnp.float32 if chunk else jnp.bfloat16,
        )
        ready = (fourth,)
        sums = ()
        for part in range(kv_parts - 1):
            sums = (last_product(chunk, [part], (last_along[part], last_across[part]), *sums),)
            ready = sums
        return fourth, sums

    begun = [begin(chunk) for chunk in range(len(chunks))]
    rights = (last_along[-1], last_across[-1])
    last = [kv_parts - 1]
    fourth, sums = begun[0]
    fifth = last_product(0, last, rights, *sums, dtype=jnp.bfloat16)
    if tp_count == 2:
        other_fourth = swap(after(fourth, fifth), "tp")
        other_fifth = swap(fifth, "tp")
        fourth, sums = begun[1]
        ready = (other_fifth,)
        fifth = last_product(1, last, rights, *sums, other_fifth, dtype=jnp.bfloat16)
        fourth = (fourth + other_fourth.astype(jnp.float32)).astype(jnp.bfloat16)
    total = jnp.concatenate([fourth, fifth], axis=1)
    shares = shares_of(total, masks)[1]
    for mask in masks:
        hand_out(mask, shares[mask], pair_columns(4, 6))
    projected = place(pieces, segments, offsets, inst_count * own_cols)
    return (projected, cache)


def solution(mesh):
    return jax.shard_map(
        per_device,
        mesh=mesh,
        in_specs=(
            P(("grp", "inst"), "tp"),
            P(("grp", "inst"), None),
            P("tp", "inst"),
            P(("grp", "inst"), None),
            P("grp"),
            P("grp", None),
        ),
        out_specs=(P(("grp", "inst", "tp"), None), P(("grp", "inst"), None, "tp")),
        check_vma=False,
    )
```

```python
import functools

import jax
import jax.numpy as jnp
from jax import lax
from jax.experimental import pallas as pl
from jax.experimental.pallas import tpu as pltpu
from jax.sharding import PartitionSpec as P

NH = 96
KVH = 8
HD = 128
PAGE = 16
OWNERS = 4
REQ_INST = 4
MAXLEN = 256
QUARTERS = 4
ROWS = 128
LOG2E = 1.4426950408889634

SIDE, NEXT, FAR = 1, 2, 4
MASKS = (0, NEXT, SIDE, NEXT | SIDE)
WIDTH = 128
LIGHT = pl.CostEstimate(flops=0, bytes_accessed=0, transcendentals=0)


def attention_kernel(info, q_ref, k_ref, v_ref, o_ref, *, heads, row_blocks, window):
    for block in range(row_blocks):
        place = info[0] * row_blocks + block
        first = pl.multiple_of(jnp.maximum(place - (window // ROWS - 1), 0) * ROWS, ROWS)
        row = place * ROWS + lax.broadcasted_iota(jnp.int32, (ROWS, window), 0)
        col = first + lax.broadcasted_iota(jnp.int32, (ROWS, window), 1)
        begin = jnp.zeros_like(row)
        for j in range(REQ_INST):
            begin = jnp.where(row >= info[2 + j], info[2 + j], begin)
        bias = jnp.where((col <= row) & (col >= begin), 0.0, -1e30)
        keys = k_ref[pl.ds(first, window), :]
        vals = v_ref[pl.ds(first, window), :]
        vals = jnp.concatenate([vals, jnp.ones_like(vals)], axis=1)
        rows = slice(block * ROWS, (block + 1) * ROWS)
        for head in range(heads):
            cols = slice(head * HD, (head + 1) * HD)
            scores = lax.dot_general(
                q_ref[rows, cols], keys, (((1,), (1,)), ((), ())),
                preferred_element_type=jnp.float32,
            )
            scores = scores * (LOG2E / HD**0.5) + bias
            expo = jnp.exp2(scores - jnp.max(scores, axis=1, keepdims=True))
            mixed = jnp.dot(expo.astype(jnp.bfloat16), vals, preferred_element_type=jnp.float32)
            o_ref[rows, cols] = (mixed[:, :HD] / mixed[:, HD:]).astype(jnp.bfloat16)


def attention(queries, keys_values, ends, first_kv, chunk, chunk_rows, part, parts):
    tok_rows, width = queries.shape
    local_heads = width // HD
    kv_heads = max(1, local_heads // (NH // KVH))
    heads = local_heads // kv_heads
    steps = kv_heads // parts
    window = min(ROWS + MAXLEN, tok_rows)
    first_kv = first_kv + part * steps
    info = jnp.concatenate([jnp.stack([chunk, first_kv]).astype(jnp.int32), ends])
    return pl.pallas_call(
        functools.partial(
            attention_kernel, heads=heads, row_blocks=chunk_rows // ROWS, window=window
        ),
        grid_spec=pltpu.PrefetchScalarGridSpec(
            num_scalar_prefetch=1,
            grid=(steps,),
            in_specs=[
                pl.BlockSpec(
                    (chunk_rows, heads * HD), lambda g, info: (info[0], part * steps + g)
                ),
                pl.BlockSpec((tok_rows, HD), lambda g, info: (0, 2 * (info[1] + g))),
                pl.BlockSpec((tok_rows, HD), lambda g, info: (0, 2 * (info[1] + g) + 1)),
            ],
            out_specs=pl.BlockSpec((chunk_rows, heads * HD), lambda g, info: (0, g)),
        ),
        out_shape=jax.ShapeDtypeStruct((chunk_rows, width // parts), jnp.bfloat16),
        compiler_params=pltpu.CompilerParams(vmem_limit_bytes=32 << 20),
        cost_estimate=LIGHT,
        name="attention",
    )(info, queries, keys_values, keys_values)


def place_kernel(offsets, *refs, segments):
    out = refs[-1]
    for n, (source, at, width) in enumerate(segments):
        start = pl.multiple_of(offsets[n], 128)
        out[:, pl.ds(start, width)] = refs[source][:, at : at + width]


def place(pieces, segments, offsets, columns):
    rows = pieces[0].shape[0]
    block = 64 if rows % 64 == 0 else rows
    return pl.pallas_call(
        functools.partial(place_kernel, segments=segments),
        grid_spec=pltpu.PrefetchScalarGridSpec(
            num_scalar_prefetch=1,
            grid=(rows // block,),
            in_specs=[
                pl.BlockSpec((block, piece.shape[1]), lambda i, offsets: (i, 0))
                for piece in pieces
            ],
            out_specs=pl.BlockSpec((block, columns), lambda i, offsets: (i, 0)),
        ),
        out_shape=jax.ShapeDtypeStruct((rows, columns), pieces[0].dtype),
        compiler_params=pltpu.CompilerParams(vmem_limit_bytes=32 << 20),
        cost_estimate=LIGHT,
        name="place",
    )(jnp.stack(offsets).astype(jnp.int32), *pieces)


def cut_kernel(places, weight_ref, o_ref):
    o_ref[...] = weight_ref[...]


def cut_out(weight, row, height, column, width, block):
    return pl.pallas_call(
        cut_kernel,
        grid_spec=pltpu.PrefetchScalarGridSpec(
            num_scalar_prefetch=1,
            grid=(height // block,),
            in_specs=[pl.BlockSpec((block, width), lambda n, places: (places[0] + n, places[1]))],
            out_specs=pl.BlockSpec((block, width), lambda n, places: (n, 0)),
        ),
        out_shape=jax.ShapeDtypeStruct((height, width), weight.dtype),
        compiler_params=pltpu.CompilerParams(vmem_limit_bytes=16 << 20),
        cost_estimate=LIGHT,
        name="cut",
    )(jnp.stack([jnp.int32(row // block), column // width]).astype(jnp.int32), weight)


def cache_kernel(page_of, pages_ref, o_ref):
    slots = o_ref.shape[0]
    first = pl.program_id(0) * slots
    for n in range(slots):
        page = page_of[first + n]
        start = pl.multiple_of(jnp.maximum(page, 0) * PAGE, PAGE)
        rows = pages_ref[pl.ds(start, PAGE), :]
        o_ref[n] = jnp.where(page >= 0, rows, jnp.zeros_like(rows))


def cache_of(pages, page_of):
    rows, width = pages.shape
    count = page_of.shape[0]
    block = 16 if count % 16 == 0 else count
    return pl.pallas_call(
        cache_kernel,
        grid_spec=pltpu.PrefetchScalarGridSpec(
            num_scalar_prefetch=1,
            grid=(count // block,),
            in_specs=[pl.BlockSpec((rows, width), lambda i, page_of: (0, 0))],
            out_specs=pl.BlockSpec((block, PAGE, width), lambda i, page_of: (i, 0, 0)),
        ),
        out_shape=jax.ShapeDtypeStruct((count, PAGE, width), pages.dtype),
        compiler_params=pltpu.CompilerParams(vmem_limit_bytes=32 << 20),
        cost_estimate=LIGHT,
        name="cache",
    )(page_of, pages)


def hop(array, mask):
    count = lax.axis_size("inst")
    return lax.ppermute(array, "inst", [(i, i ^ mask) for i in range(count)])


def swap(array, axis):
    return lax.ppermute(array, axis, [(0, 1), (1, 0)])


def product_kernel(*refs, masks, chunks, segments, groups, summands):
    step = pl.program_id(0)
    parts = 1 + max(part for part, _, _ in segments)
    count = masks * chunks * parts
    left_refs, rest = refs[:count], refs[count:]
    sources, wide = [], []
    for _, size in groups:
        taken = max(size, 1)
        if size:
            sources.extend(rest[:taken])
        wide.append(None if size else rest[0])
        rest = rest[taken:]
    others, rest = rest[: summands * chunks], rest[summands * chunks :]
    outs, rest = rest[:chunks], rest[chunks:]
    held, rest = rest[: len(sources)], rest[len(sources) :]
    lefts, sems = rest[:-1], rest[-1]
    rows = left_refs[0].shape[0]

    copies, narrow_copies = [], []
    for mask in range(masks):
        mine = []
        for chunk in range(chunks):
            block = mask * chunks + chunk
            for n, (part, start, size) in enumerate(segments):
                mine.append(
                    pltpu.make_async_copy(
                        left_refs[block * parts + part].at[:, start : start + size],
                        lefts[n].at[block * rows : (block + 1) * rows, :],
                        sems.at[block * len(segments) + n],
                    )
                )
        copies.append(mine)
    used = masks * chunks * len(segments)
    for n, ref in enumerate(sources):
        narrow_copies.append(pltpu.make_async_copy(ref, held[n], sems.at[used + n]))

    def start():
        mine = [copy for group in copies for copy in group]
        for copy in narrow_copies + mine if groups[0][1] else mine + narrow_copies:
            copy.start()

    def compute(rights, arrived, first, alone):
        for copy in arrived:
            copy.wait()
        for mask in range(masks):
            if first == 0:
                for copy in copies[mask]:
                    if alone:
                        copy.wait()
                    else:
                        pl.when(step == 0)(copy.wait)
            total, at = None, 0
            span = slice(mask * chunks * rows, (mask + 1) * chunks * rows)
            for n, (_, _, size) in enumerate(segments):
                right = jnp.concatenate([ref[at : at + size, :] for ref in rights], axis=1)
                term = jnp.dot(lefts[n][span, :], right, preferred_element_type=jnp.float32)
                total = term if total is None else total + term
                at += size
            span = slice(mask * rows, (mask + 1) * rows)
            for chunk in range(chunks):
                result = total[chunk * rows : (chunk + 1) * rows, :]
                for other in others[chunk::chunks]:
                    result = result + other[span, :].astype(jnp.float32)
                outs[chunk][span, :] = result.astype(outs[chunk].dtype)

    if sum(steps for steps, _ in groups) == 1:
        start()
    else:
        pl.when(step == 0)(start)
    first, at = 0, 0
    for (steps, size), ref in zip(groups, wide):
        rights = held[at : at + size] if size else [ref]
        body = functools.partial(
            compute, rights, narrow_copies[at : at + size], first, steps == 1
        )
        at += size
        if len(groups) == 1:
            body()
        else:
            pl.when((step >= first) & (step < first + steps))(body)
        first += steps


def product(blocks, rights, span, summands=(), dtype=jnp.bfloat16):
    masks, chunks, parts = len(blocks), len(blocks[0]), len(blocks[0][0])
    rows, depth = blocks[0][0][0].shape
    segments = []
    for part in range(parts):
        low, high = max(span[0] - part * depth, 0), min(span[1] - part * depth, depth)
        if low < high:
            segments.append((part, low, high - low))
    skipped = segments[0][0]
    segments = [(part - skipped, low, size) for part, low, size in segments]
    block = 4 * WIDTH
    anywhere = pl.BlockSpec(memory_space=pl.ANY)
    operands = [
        array
        for mask in blocks
        for chunk in mask
        for array in chunk[skipped : skipped + 1 + segments[-1][0]]
    ]
    specs = [anywhere] * len(operands)
    copies = masks * chunks * len(segments)
    groups, held, first = [], [], 0
    for right in rights:
        if isinstance(right, tuple):
            steps = 1
            operands += right
            specs += [anywhere] * len(right)
            held += [pltpu.VMEM(piece.shape, piece.dtype) for piece in right]
            groups.append((1, len(right)))
        else:
            steps = right.shape[1] // block
            operands.append(right)
            specs.append(
                pl.BlockSpec(
                    (right.shape[0], block),
                    lambda n, first=first, steps=steps: (0, jnp.clip(n - first, 0, steps - 1)),
                )
            )
            groups.append((steps, 0))
        first += steps
    out_spec = pl.BlockSpec((rows * masks, block), lambda n: (0, n))
    for summand in summands:
        operands += summand
        specs += [out_spec] * chunks
    scratch = [
        pltpu.VMEM((masks * chunks * rows, size), operands[0].dtype) for _, _, size in segments
    ]
    return pl.pallas_call(
        functools.partial(
            product_kernel, masks=masks, chunks=chunks, segments=segments, groups=groups,
            summands=len(summands),
        ),
        grid=(first,),
        in_specs=specs,
        out_specs=[out_spec] * chunks,
        out_shape=[jax.ShapeDtypeStruct((rows * masks, first * block), dtype)] * chunks,
        scratch_shapes=held + scratch + [pltpu.SemaphoreType.DMA((copies + len(held),))],
        compiler_params=pltpu.CompilerParams(vmem_limit_bytes=60 << 20),
        cost_estimate=LIGHT,
        name="product",
    )(*operands)


def after(array, *earlier):
    return lax.optimization_barrier((array,) + earlier)[0]


def data_pages(tok_rows):
    span = PAGE * OWNERS
    return (tok_rows + REQ_INST * (span - 1)) // span


def packing(lens, residue):
    page_counts = (lens + (PAGE - 1)) // PAGE
    counts = jnp.maximum(page_counts - residue + (OWNERS - 1), 0) // OWNERS
    return counts, jnp.cumsum(counts, axis=-1) - counts


def packed_pages(held, lens, residues, tok_rows):
    limit = data_pages(tok_rows)
    starts = jnp.cumsum(lens) - lens
    residues = jnp.stack(residues)[:, None]
    counts, firsts = packing(lens[None, :], residues)
    slot = jnp.arange(limit + 1, dtype=jnp.int32)
    step = slot[None, :, None] - firsts[:, None, :]
    mine = (step >= 0) & (step < counts[:, None, :])
    offset = (step * OWNERS + residues[:, :, None]) * PAGE
    base = jnp.sum(jnp.where(mine, starts[None, None, :] + offset, 0), axis=2)
    live = jnp.sum(jnp.where(mine, jnp.minimum(lens[None, None, :] - offset, PAGE), 0), axis=2)
    base = jnp.where(slot[None, :] == limit, tok_rows, base)
    live = jnp.where(slot[None, :] == limit, PAGE, live)
    within = jnp.arange(PAGE, dtype=jnp.int32)
    row = jnp.where(
        within[None, None, :] < live[:, :, None], base[:, :, None] + within[None, None, :], -1
    ).reshape(-1)
    chosen = row[:, None] == jnp.arange(held.shape[0], dtype=jnp.int32)[None, :]
    pages = jnp.dot(chosen.astype(held.dtype), held, preferred_element_type=jnp.float32)
    return pages.astype(held.dtype).reshape(residues.shape[0], (limit + 1) * PAGE, held.shape[1])


def slot_pages(lens, placement, page_table, block_of, limit):
    inst_here = lax.axis_index("inst")
    residue = inst_here % OWNERS
    requests = page_table.shape[0]
    slot_count = requests * QUARTERS
    counts, firsts = packing(lens, residue)
    slots = lax.dynamic_index_in_dim(
        page_table.reshape(requests, QUARTERS, OWNERS), residue, axis=2, keepdims=False
    )
    step = jnp.arange(QUARTERS, dtype=jnp.int32)
    valid = (placement == inst_here // OWNERS)[:, None] & (step[None, :] < counts.reshape(-1)[:, None])
    page = (firsts + block_of[:, None] * (limit + 1)).reshape(-1)[:, None] + step[None, :]
    target = jnp.where(valid, slots, slot_count).reshape(-1)
    match = target[None, :] == jnp.arange(slot_count, dtype=jnp.int32)[:, None]
    return jnp.sum(jnp.where(match, page.reshape(-1)[None, :] + 1, 0), axis=1) - 1


def per_device(queries, keys_values, out_weight, lengths, placement, page_table):
    tok_rows = queries.shape[0]
    tp_count = lax.axis_size("tp")
    tp_here = lax.axis_index("tp")
    inst_count = lax.axis_size("inst")
    inst_here = lax.axis_index("inst")
    grp_here = lax.axis_index("grp")
    side_here = inst_here % 2
    next_here = inst_here // NEXT % 2
    local_heads = queries.shape[1] // HD
    first_kv = tp_here * local_heads // (NH // KVH)
    ends = jnp.cumsum(lengths[0])
    depth, own_cols = out_weight.shape
    half_cols = own_cols // 2
    kv_width = keys_values.shape[1] // tp_count

    narrow = 4
    parts = 4 if depth % 512 == 0 else 2
    spans = [(0, depth // 2)] + [
        (n * depth // parts, (n + 1) * depth // parts) for n in range(parts // 2, parts)
    ]
    cuts = [(0, depth, n * WIDTH, WIDTH) for n in range(narrow)] + [
        (low, high - low, narrow * WIDTH, half_cols - narrow * WIDTH) for low, high in spans
    ]

    gate = ()

    def gated(array):
        return after(array, *gate) if gate else array

    def cut(n, *earlier):
        weight = after(out_weight, *earlier) if earlier else out_weight
        row, height, column, width = cuts[n]
        return cut_out(
            weight, row, height, grp_here * half_cols + column, width, depth // parts
        )

    pieces, segments, offsets = [], [], []
    own_columns = [(own_cols, lambda inst: inst * own_cols)]

    def far_columns(first, last):
        return [
            (
                cuts[n][3],
                lambda inst, n=n, half=half: (inst ^ FAR) * own_cols + half * half_cols + cuts[n][2],
            )
            for n in range(first, last)
            for half in (grp_here, 1 - grp_here)
        ]

    def hand_out(mask, share, columns):
        at = 0
        for width, column_of in columns:
            segments.append((len(pieces), at, width))
            offsets.append(column_of(inst_here ^ mask))
            at += width
        pieces.append(hop(share, mask) if mask else share)
        return pieces[-1]

    kv_parts = 2 if local_heads % (2 * (NH // KVH)) == 0 else 1
    blocks = {mask: [] for mask in MASKS}

    def products(masks, rights, span=(0, depth), summands=(), dtype=jnp.bfloat16):
        groups = []
        for mask in masks:
            rows = blocks[mask]
            groups.append([rows[n : n + kv_parts] for n in range(0, len(rows), kv_parts)])
        groups[0][0] = [gated(array) for array in groups[0][0]]
        return product(groups, rights, span, summands, dtype)

    def finish(totals, masks, *earlier):
        given = after(totals[0], *earlier) if earlier else totals[0]
        rows = given.shape[0] // len(masks)
        if tp_count == 2:
            other = swap(given, "tp")
            total = (totals[1].astype(jnp.float32) + other.astype(jnp.float32)).astype(other.dtype)
            return {mask: total[n * rows : (n + 1) * rows] for n, mask in enumerate(masks)}
        return {
            mask: lax.psum_scatter(
                given[n * rows : (n + 1) * rows], "tp", scatter_dimension=0, tiled=True
            )
            for n, mask in enumerate(masks)
        }

    sliced, along, across = [cut(0)], [], []
    along.append(hop(sliced[0], FAR))
    held = lax.dynamic_slice_in_dim(
        after(keys_values, sliced[0]), tp_here * kv_width, kv_width, 1
    )
    lens_rows = jnp.zeros((PAGE, kv_width), held.dtype)
    lens_rows = lens_rows.at[0, :REQ_INST].set(lengths[0].astype(held.dtype))
    held = jnp.concatenate([held, lens_rows], axis=0)
    held_far = hop(held, FAR)
    chunks = [1 - tp_here, tp_here] if tp_count == 2 else [jnp.int32(0)]
    own = blocks[0]
    ready = held
    for chunk in chunks:
        for part in range(kv_parts):
            ready = attention(
                after(queries, ready), keys_values, ends, first_kv, chunk,
                tok_rows // len(chunks), part, kv_parts,
            )
            own.append(ready)

    def spread(name, arrays, mask):
        sent = [hop(gated(array), mask) for array in arrays]
        blocks[name] += sent
        return tuple(sent)

    moved = spread(NEXT, own[:1], NEXT) + spread(SIDE, own[:2], SIDE)
    for n in range(1, len(cuts)):
        ready = cut(n, ready)
        sliced.append(ready)

    held_far = after(held_far, ready)
    pages_given, pages_kept = (
        jnp.stack(
            [
                packed_pages(rows, lens, residues, tok_rows)
                for rows, lens in (
                    (held, lengths[0]),
                    (held_far, held_far[tok_rows, :REQ_INST].astype(jnp.int32)),
                )
            ]
        )
        for residues in ([1 - side_here, 3 - side_here], [side_here, 2 + side_here])
    )
    gate = moved + (along[0], pages_given, pages_kept)

    def weights():
        n = len(across)
        across.append(swap(gated(along[n]), "grp"))
        along.append(hop(gated(sliced[n + 1]), FAR))
        return (across[-1], along[-1])

    moved = weights() + spread(NEXT, own[1:2], NEXT) + spread(SIDE, own[2:], SIDE)
    own_shares = finish(products((0,), [out_weight]), (0,), moved[0])
    gate = moved + (own_shares[0],)

    near = blocks[NEXT]
    moved = weights() + spread(NEXT, own[2:3], NEXT) + spread(NEXT | SIDE, near[:2], SIDE)
    own_shares.update(finish(products((SIDE,), [out_weight]), (SIDE,), moved[0]))
    gate = moved + (own_shares[SIDE],)

    def two_pairs(n):
        return (along[n], across[n], along[n + 1], across[n + 1])

    moved = weights() + spread(NEXT, own[3:], NEXT) + spread(NEXT | SIDE, near[2:3], SIDE)
    pages_side = hop(gated(pages_given), SIDE)
    shares = finish(products((0, SIDE), [two_pairs(0)]), (0, SIDE), moved[0])
    gate = moved + (pages_side, shares[0])

    first_columns = own_columns + far_columns(0, 2)
    moved = weights() + spread(NEXT | SIDE, near[3:], SIDE)
    side_share = jnp.concatenate([own_shares[SIDE], shares[SIDE]], axis=1)
    hand_out(0, own_shares[0], own_columns)
    hand_out(0, shares[0], far_columns(0, 2))
    pages = gated(jnp.concatenate([pages_kept, pages_side], axis=0))
    pages_next = hop(
        lax.dynamic_index_in_dim(pages, 1 - next_here, axis=1, keepdims=False), NEXT
    )
    pages = lax.dynamic_index_in_dim(pages, next_here, axis=1, keepdims=False)
    begun = products((NEXT,), [out_weight, two_pairs(0)])
    shares = finish(begun, (NEXT,))
    begun_near = products((SIDE, NEXT, 0), [after(two_pairs(2), begun[0])])
    gate = moved + (pages_next, begun_near[0])

    moved = weights() + (
        hand_out(NEXT, gated(shares[NEXT]), first_columns),
        hand_out(SIDE, gated(side_share), first_columns),
    )
    begun = products((NEXT | SIDE,), [out_weight, two_pairs(0), two_pairs(2)])
    near_shares = finish(begun_near, (SIDE, NEXT, 0), begun[0], moved[1])
    far_shares = finish(begun, (NEXT | SIDE,), begun[0], moved[1])
    gate = moved
    for n in range(narrow + 2, len(cuts)):
        moved += weights()
        gate = moved
    far_share = hand_out(
        NEXT | SIDE, far_shares[NEXT | SIDE], own_columns + far_columns(0, 4)
    )
    moved += tuple(
        hand_out(mask, near_shares[mask], far_columns(2, 4)) for mask in (NEXT, SIDE, 0)
    )
    pages = jnp.concatenate([pages, after(pages_next, near_shares[0])], axis=0)
    order = [mask ^ far for mask in (0, SIDE) for far in (0, FAR)]
    order = order + [at ^ NEXT for at in order]
    block_of = jnp.asarray([order.index(i) for i in range(inst_count)], jnp.int32)
    block_of = jnp.take(block_of, jnp.arange(inst_count, dtype=jnp.int32) ^ inst_here)
    limit = data_pages(tok_rows)
    lens = jnp.take(pages[:, limit * PAGE, :REQ_INST].astype(jnp.int32), block_of, axis=0)
    page_of = slot_pages(lens, placement, page_table, block_of, limit)
    cache = cache_of(pages.reshape(-1, kv_width), page_of)
    gate = moved + (cache, far_shares[NEXT | SIDE])

    across.append(swap(gated(along[-1]), "grp"))
    masks = (NEXT | SIDE, NEXT, SIDE, 0)
    sums = []
    for n, span in enumerate(spans):
        last = n == len(spans) - 1
        if last:
            gate = (far_share,)
        rights = (along[narrow + n], across[narrow + n])
        sums = [
            products(masks, [rights], span, sums, jnp.bfloat16 if last else jnp.float32)
        ]
    sums = sums[0]
    shares = finish(sums, masks)
    for mask in masks:
        hand_out(mask, shares[mask], far_columns(narrow, narrow + 1))
    projected = place(pieces, segments, offsets, inst_count * own_cols)
    return (projected, cache)


def solution(mesh):
    return jax.shard_map(
        per_device,
        mesh=mesh,
        in_specs=(
            P(("grp", "inst"), "tp"),
            P(("grp", "inst"), None),
            P("tp", "inst"),
            P(("grp", "inst"), None),
            P("grp"),
            P("grp", None),
        ),
        out_specs=(P(("grp", "inst", "tp"), None), P(("grp", "inst"), None, "tp")),
        check_vma=False,
    )
```

```python
import functools

import jax
import jax.numpy as jnp
from jax import lax
from jax.experimental import pallas as pl
from jax.experimental.pallas import tpu as pltpu
from jax.sharding import PartitionSpec as P

NH = 96
KVH = 8
HD = 128
PAGE = 16
OWNERS = 4
REQ_INST = 4
MAXLEN = 256
QUARTERS = 4
ROWS = 128
LOG2E = 1.4426950408889634

SIDE, NEXT, FAR = 1, 2, 4
MASKS = (0, NEXT, SIDE, NEXT | SIDE)
WIDTH = 128
LIGHT = pl.CostEstimate(flops=0, bytes_accessed=0, transcendentals=0)


def attention_kernel(info, q_ref, k_ref, v_ref, o_ref, *, heads, row_blocks, window):
    for block in range(row_blocks):
        place = info[0] * row_blocks + block
        first = pl.multiple_of(jnp.maximum(place - (window // ROWS - 1), 0) * ROWS, ROWS)
        row = place * ROWS + lax.broadcasted_iota(jnp.int32, (ROWS, window), 0)
        col = first + lax.broadcasted_iota(jnp.int32, (ROWS, window), 1)
        begin = jnp.zeros_like(row)
        for j in range(REQ_INST):
            begin = jnp.where(row >= info[2 + j], info[2 + j], begin)
        bias = jnp.where((col <= row) & (col >= begin), 0.0, -1e30)
        keys = k_ref[pl.ds(first, window), :]
        vals = v_ref[pl.ds(first, window), :]
        vals = jnp.concatenate([vals, jnp.ones_like(vals)], axis=1)
        rows = slice(block * ROWS, (block + 1) * ROWS)
        for head in range(heads):
            cols = slice(head * HD, (head + 1) * HD)
            scores = lax.dot_general(
                q_ref[rows, cols], keys, (((1,), (1,)), ((), ())),
                preferred_element_type=jnp.float32,
            )
            scores = scores * (LOG2E / HD**0.5) + bias
            expo = jnp.exp2(scores - jnp.max(scores, axis=1, keepdims=True))
            mixed = jnp.dot(expo.astype(jnp.bfloat16), vals, preferred_element_type=jnp.float32)
            o_ref[rows, cols] = (mixed[:, :HD] / mixed[:, HD:]).astype(jnp.bfloat16)


def attention(queries, keys_values, ends, first_kv, chunk, chunk_rows, part, parts):
    tok_rows, width = queries.shape
    local_heads = width // HD
    kv_heads = max(1, local_heads // (NH // KVH))
    heads = local_heads // kv_heads
    steps = kv_heads // parts
    window = min(ROWS + MAXLEN, tok_rows)
    first_kv = first_kv + part * steps
    info = jnp.concatenate([jnp.stack([chunk, first_kv]).astype(jnp.int32), ends])
    return pl.pallas_call(
        functools.partial(
            attention_kernel, heads=heads, row_blocks=chunk_rows // ROWS, window=window
        ),
        grid_spec=pltpu.PrefetchScalarGridSpec(
            num_scalar_prefetch=1,
            grid=(steps,),
            in_specs=[
                pl.BlockSpec(
                    (chunk_rows, heads * HD), lambda g, info: (info[0], part * steps + g)
                ),
                pl.BlockSpec((tok_rows, HD), lambda g, info: (0, 2 * (info[1] + g))),
                pl.BlockSpec((tok_rows, HD), lambda g, info: (0, 2 * (info[1] + g) + 1)),
            ],
            out_specs=pl.BlockSpec((chunk_rows, heads * HD), lambda g, info: (0, g)),
        ),
        out_shape=jax.ShapeDtypeStruct((chunk_rows, width // parts), jnp.bfloat16),
        compiler_params=pltpu.CompilerParams(vmem_limit_bytes=60 << 20),
        cost_estimate=LIGHT,
        name="attention",
    )(info, queries, keys_values, keys_values)


def place_kernel(offsets, *refs, segments):
    out = refs[-1]
    for n, (source, at, width) in enumerate(segments):
        start = pl.multiple_of(offsets[n], 128)
        out[:, pl.ds(start, width)] = refs[source][:, at : at + width]


def place(pieces, segments, offsets, columns):
    rows = pieces[0].shape[0]
    block = 64 if rows % 64 == 0 else rows
    return pl.pallas_call(
        functools.partial(place_kernel, segments=segments),
        grid_spec=pltpu.PrefetchScalarGridSpec(
            num_scalar_prefetch=1,
            grid=(rows // block,),
            in_specs=[
                pl.BlockSpec((block, piece.shape[1]), lambda i, offsets: (i, 0))
                for piece in pieces
            ],
            out_specs=pl.BlockSpec((block, columns), lambda i, offsets: (i, 0)),
        ),
        out_shape=jax.ShapeDtypeStruct((rows, columns), pieces[0].dtype),
        compiler_params=pltpu.CompilerParams(vmem_limit_bytes=60 << 20),
        cost_estimate=LIGHT,
        name="place",
    )(jnp.stack(offsets).astype(jnp.int32), *pieces)


def cut_kernel(places, weight_ref, o_ref):
    o_ref[...] = weight_ref[...]


def cut_out(weight, row, height, column, width, block):
    return pl.pallas_call(
        cut_kernel,
        grid_spec=pltpu.PrefetchScalarGridSpec(
            num_scalar_prefetch=1,
            grid=(height // block,),
            in_specs=[pl.BlockSpec((block, width), lambda n, places: (places[0] + n, places[1]))],
            out_specs=pl.BlockSpec((block, width), lambda n, places: (n, 0)),
        ),
        out_shape=jax.ShapeDtypeStruct((height, width), weight.dtype),
        compiler_params=pltpu.CompilerParams(vmem_limit_bytes=60 << 20),
        cost_estimate=LIGHT,
        name="cut",
    )(jnp.stack([jnp.int32(row // block), column // width]).astype(jnp.int32), weight)


def cache_kernel(page_of, near_ref, far_ref, o_ref):
    slots = o_ref.shape[0]
    first = pl.program_id(0) * slots
    count = near_ref.shape[0] // PAGE
    for n in range(slots):
        page = page_of[first + n]
        near = pl.multiple_of(jnp.clip(page, 0, count - 1) * PAGE, PAGE)
        far = pl.multiple_of(jnp.clip(page - count, 0, count - 1) * PAGE, PAGE)
        rows = jnp.where(
            page < count, near_ref[pl.ds(near, PAGE), :], far_ref[pl.ds(far, PAGE), :]
        )
        o_ref[n] = jnp.where(page >= 0, rows, jnp.zeros_like(rows))


def cache_of(near, far, page_of):
    rows, width = near.shape
    count = page_of.shape[0]
    block = 16 if count % 16 == 0 else count
    return pl.pallas_call(
        cache_kernel,
        grid_spec=pltpu.PrefetchScalarGridSpec(
            num_scalar_prefetch=1,
            grid=(count // block,),
            in_specs=[pl.BlockSpec((rows, width), lambda i, page_of: (0, 0))] * 2,
            out_specs=pl.BlockSpec((block, PAGE, width), lambda i, page_of: (i, 0, 0)),
        ),
        out_shape=jax.ShapeDtypeStruct((count, PAGE, width), near.dtype),
        compiler_params=pltpu.CompilerParams(vmem_limit_bytes=60 << 20),
        cost_estimate=LIGHT,
        name="cache",
    )(page_of, near, far)


def hop(array, mask):
    count = lax.axis_size("inst")
    return lax.ppermute(array, "inst", [(i, i ^ mask) for i in range(count)])


def swap(array, axis):
    return lax.ppermute(array, axis, [(0, 1), (1, 0)])


def product_kernel(*refs, masks, chunks, segments, groups, summands):
    step = pl.program_id(0)
    parts = 1 + max(part for part, _, _ in segments)
    count = masks * chunks * parts
    left_refs, rest = refs[:count], refs[count:]
    sources, wide = [], []
    for _, size in groups:
        taken = max(size, 1)
        if size:
            sources.extend(rest[:taken])
        wide.append(None if size else rest[0])
        rest = rest[taken:]
    others, rest = rest[: summands * chunks], rest[summands * chunks :]
    outs, rest = rest[:chunks], rest[chunks:]
    held, rest = rest[: len(sources)], rest[len(sources) :]
    lefts, sems = rest[:-1], rest[-1]
    rows = left_refs[0].shape[0]

    copies, narrow_copies = [], []
    for mask in range(masks):
        mine = []
        for chunk in range(chunks):
            block = mask * chunks + chunk
            for n, (part, start, size) in enumerate(segments):
                mine.append(
                    pltpu.make_async_copy(
                        left_refs[block * parts + part].at[:, start : start + size],
                        lefts[n].at[block * rows : (block + 1) * rows, :],
                        sems.at[block * len(segments) + n],
                    )
                )
        copies.append(mine)
    used = masks * chunks * len(segments)
    for n, ref in enumerate(sources):
        narrow_copies.append(pltpu.make_async_copy(ref, held[n], sems.at[used + n]))

    def start():
        mine = [copy for group in copies for copy in group]
        for copy in narrow_copies + mine if groups[0][1] else mine + narrow_copies:
            copy.start()

    def compute(rights, arrived, first, alone):
        for copy in arrived:
            copy.wait()
        for mask in range(masks):
            if first == 0:
                for copy in copies[mask]:
                    if alone:
                        copy.wait()
                    else:
                        pl.when(step == 0)(copy.wait)
            total, at = None, 0
            span = slice(mask * chunks * rows, (mask + 1) * chunks * rows)
            for n, (_, _, size) in enumerate(segments):
                right = jnp.concatenate([ref[at : at + size, :] for ref in rights], axis=1)
                term = jnp.dot(lefts[n][span, :], right, preferred_element_type=jnp.float32)
                total = term if total is None else total + term
                at += size
            span = slice(mask * rows, (mask + 1) * rows)
            for chunk in range(chunks):
                result = total[chunk * rows : (chunk + 1) * rows, :]
                for other in others[chunk::chunks]:
                    result = result + other[span, :].astype(jnp.float32)
                outs[chunk][span, :] = result.astype(outs[chunk].dtype)

    if sum(steps for steps, _ in groups) == 1:
        start()
    else:
        pl.when(step == 0)(start)
    first, at = 0, 0
    for (steps, size), ref in zip(groups, wide):
        rights = held[at : at + size] if size else [ref]
        body = functools.partial(
            compute, rights, narrow_copies[at : at + size], first, steps == 1
        )
        at += size
        if len(groups) == 1:
            body()
        else:
            pl.when((step >= first) & (step < first + steps))(body)
        first += steps


def product(blocks, rights, span, summands=(), dtype=jnp.bfloat16):
    masks, chunks, parts = len(blocks), len(blocks[0]), len(blocks[0][0])
    rows, depth = blocks[0][0][0].shape
    segments = []
    for part in range(parts):
        low, high = max(span[0] - part * depth, 0), min(span[1] - part * depth, depth)
        if low < high:
            segments.append((part, low, high - low))
    skipped = segments[0][0]
    segments = [(part - skipped, low, size) for part, low, size in segments]
    block = 4 * WIDTH
    anywhere = pl.BlockSpec(memory_space=pl.ANY)
    operands = [
        array
        for mask in blocks
        for chunk in mask
        for array in chunk[skipped : skipped + 1 + segments[-1][0]]
    ]
    specs = [anywhere] * len(operands)
    copies = masks * chunks * len(segments)
    groups, held, first = [], [], 0
    for right in rights:
        if isinstance(right, tuple):
            steps = 1
            operands += right
            specs += [anywhere] * len(right)
            held += [pltpu.VMEM(piece.shape, piece.dtype) for piece in right]
            groups.append((1, len(right)))
        else:
            steps = right.shape[1] // block
            operands.append(right)
            specs.append(
                pl.BlockSpec(
                    (right.shape[0], block),
                    lambda n, first=first, steps=steps: (0, jnp.clip(n - first, 0, steps - 1)),
                )
            )
            groups.append((steps, 0))
        first += steps
    out_spec = pl.BlockSpec((rows * masks, block), lambda n: (0, n))
    for summand in summands:
        operands += summand
        specs += [out_spec] * chunks
    scratch = [
        pltpu.VMEM((masks * chunks * rows, size), operands[0].dtype) for _, _, size in segments
    ]
    return pl.pallas_call(
        functools.partial(
            product_kernel, masks=masks, chunks=chunks, segments=segments, groups=groups,
            summands=len(summands),
        ),
        grid=(first,),
        in_specs=specs,
        out_specs=[out_spec] * chunks,
        out_shape=[jax.ShapeDtypeStruct((rows * masks, first * block), dtype)] * chunks,
        scratch_shapes=held + scratch + [pltpu.SemaphoreType.DMA((copies + len(held),))],
        compiler_params=pltpu.CompilerParams(vmem_limit_bytes=60 << 20),
        cost_estimate=LIGHT,
        name="product",
    )(*operands)


def after(array, *earlier):
    return lax.optimization_barrier((array,) + earlier)[0]


def data_pages(tok_rows):
    span = PAGE * OWNERS
    return (tok_rows + REQ_INST * (span - 1)) // span


def packing(lens, residue):
    page_counts = (lens + (PAGE - 1)) // PAGE
    counts = jnp.maximum(page_counts - residue + (OWNERS - 1), 0) // OWNERS
    return counts, jnp.cumsum(counts, axis=-1) - counts


def packed_pages(held, lens, residues, tok_rows):
    limit = data_pages(tok_rows)
    starts = jnp.cumsum(lens) - lens
    residues = jnp.stack(residues)[:, None]
    counts, firsts = packing(lens[None, :], residues)
    slot = jnp.arange(limit + 1, dtype=jnp.int32)
    step = slot[None, :, None] - firsts[:, None, :]
    mine = (step >= 0) & (step < counts[:, None, :])
    offset = (step * OWNERS + residues[:, :, None]) * PAGE
    base = jnp.sum(jnp.where(mine, starts[None, None, :] + offset, 0), axis=2)
    live = jnp.sum(jnp.where(mine, jnp.minimum(lens[None, None, :] - offset, PAGE), 0), axis=2)
    base = jnp.where(slot[None, :] == limit, tok_rows, base)
    live = jnp.where(slot[None, :] == limit, PAGE, live)
    within = jnp.arange(PAGE, dtype=jnp.int32)
    row = jnp.where(
        within[None, None, :] < live[:, :, None], base[:, :, None] + within[None, None, :], -1
    ).reshape(-1)
    chosen = row[:, None] == jnp.arange(held.shape[0], dtype=jnp.int32)[None, :]
    pages = jnp.dot(chosen.astype(held.dtype), held, preferred_element_type=jnp.float32)
    return pages.astype(held.dtype).reshape(residues.shape[0], (limit + 1) * PAGE, held.shape[1])


def slot_pages(lens, placement, page_table, block_of, limit):
    inst_here = lax.axis_index("inst")
    residue = inst_here % OWNERS
    requests = page_table.shape[0]
    slot_count = requests * QUARTERS
    counts, firsts = packing(lens, residue)
    slots = lax.dynamic_index_in_dim(
        page_table.reshape(requests, QUARTERS, OWNERS), residue, axis=2, keepdims=False
    )
    step = jnp.arange(QUARTERS, dtype=jnp.int32)
    valid = (placement == inst_here // OWNERS)[:, None] & (step[None, :] < counts.reshape(-1)[:, None])
    page = (firsts + block_of[:, None] * (limit + 1)).reshape(-1)[:, None] + step[None, :]
    target = jnp.where(valid, slots, slot_count).reshape(-1)
    match = target[None, :] == jnp.arange(slot_count, dtype=jnp.int32)[:, None]
    return jnp.sum(jnp.where(match, page.reshape(-1)[None, :] + 1, 0), axis=1) - 1


def per_device(queries, keys_values, out_weight, lengths, placement, page_table):
    tok_rows = queries.shape[0]
    tp_count = lax.axis_size("tp")
    tp_here = lax.axis_index("tp")
    inst_count = lax.axis_size("inst")
    inst_here = lax.axis_index("inst")
    grp_here = lax.axis_index("grp")
    side_here = inst_here % 2
    next_here = inst_here // NEXT % 2
    local_heads = queries.shape[1] // HD
    first_kv = tp_here * local_heads // (NH // KVH)
    ends = jnp.cumsum(lengths[0])
    depth, own_cols = out_weight.shape
    half_cols = own_cols // 2
    kv_width = keys_values.shape[1] // tp_count

    narrow = 4
    parts = 4 if depth % 512 == 0 else 2
    spans = [(0, depth // 2)] + [
        (n * depth // parts, (n + 1) * depth // parts) for n in range(parts // 2, parts)
    ]
    cuts = [(0, depth, n * WIDTH, WIDTH) for n in range(narrow)] + [
        (low, high - low, narrow * WIDTH, half_cols - narrow * WIDTH) for low, high in spans
    ]

    gate = ()

    def gated(array):
        return after(array, *gate) if gate else array

    def cut(n, *earlier):
        weight = after(out_weight, *earlier) if earlier else out_weight
        row, height, column, width = cuts[n]
        return cut_out(
            weight, row, height, grp_here * half_cols + column, width, depth // parts
        )

    pieces, segments, offsets = [], [], []
    own_columns = [(own_cols, lambda inst: inst * own_cols)]

    def far_columns(first, last):
        return [
            (
                cuts[n][3],
                lambda inst, n=n, half=half: (inst ^ FAR) * own_cols + half * half_cols + cuts[n][2],
            )
            for n in range(first, last)
            for half in (grp_here, 1 - grp_here)
        ]

    def hand_out(mask, share, columns):
        at = 0
        for width, column_of in columns:
            segments.append((len(pieces), at, width))
            offsets.append(column_of(inst_here ^ mask))
            at += width
        pieces.append(hop(share, mask) if mask else share)
        return pieces[-1]

    kv_parts = 2 if local_heads % (2 * (NH // KVH)) == 0 else 1
    blocks = {mask: [] for mask in MASKS}

    def products(masks, rights, span=(0, depth), summands=(), dtype=jnp.bfloat16):
        groups = []
        for mask in masks:
            rows = blocks[mask]
            groups.append([rows[n : n + kv_parts] for n in range(0, len(rows), kv_parts)])
        groups[0][0] = [gated(array) for array in groups[0][0]]
        return product(groups, rights, span, summands, dtype)

    def finish(totals, masks, *earlier, swaps=1):
        given = after(totals[0], *earlier) if earlier else totals[0]
        rows = given.shape[0] // len(masks)
        if tp_count == 2:
            some = given.shape[0] // swaps
            other = jnp.concatenate(
                [swap(given[n * some : (n + 1) * some], "tp") for n in range(swaps)], axis=0
            )
            total = (totals[1].astype(jnp.float32) + other.astype(jnp.float32)).astype(other.dtype)
            return {mask: total[n * rows : (n + 1) * rows] for n, mask in enumerate(masks)}
        return {
            mask: lax.psum_scatter(
                given[n * rows : (n + 1) * rows], "tp", scatter_dimension=0, tiled=True
            )
            for n, mask in enumerate(masks)
        }

    sliced, along, across = [cut(0)], [], []
    along.append(hop(sliced[0], FAR))
    chunks = [1 - tp_here, tp_here] if tp_count == 2 else [jnp.int32(0)]
    own = blocks[0]
    ready = sliced[0]
    for chunk in chunks:
        for part in range(kv_parts):
            ready = attention(
                after(queries, ready), keys_values, ends, first_kv, chunk,
                tok_rows // len(chunks), part, kv_parts,
            )
            own.append(ready)

    def spread(name, arrays, mask):
        sent = [hop(gated(array), mask) for array in arrays]
        blocks[name] += sent
        return tuple(sent)

    moved = spread(NEXT, own[:1], NEXT) + spread(SIDE, own[:2], SIDE)
    for n in range(1, len(cuts)):
        ready = cut(n, ready)
        sliced.append(ready)

    seen = jnp.sum(along[0].astype(jnp.float32), axis=0)
    gate = moved + (along[0], seen, ready)

    def weights():
        n = len(across)
        across.append(swap(gated(along[n]), "grp"))
        along.append(hop(gated(sliced[n + 1]), FAR))
        return (across[-1], along[-1])

    moved = weights() + spread(NEXT, own[1:2], NEXT) + spread(SIDE, own[2:], SIDE)
    held = lax.dynamic_slice_in_dim(
        gated(keys_values), tp_here * kv_width, kv_width, 1
    )
    lens_rows = jnp.zeros((PAGE, kv_width), held.dtype)
    lens_rows = lens_rows.at[0, :REQ_INST].set(lengths[0].astype(held.dtype))
    held = jnp.concatenate([held, lens_rows], axis=0)
    pages = packed_pages(
        held, lengths[0], [1 - side_here, 3 - side_here, side_here, 2 + side_here], tok_rows
    )
    pages_given, pages_kept = pages[None, :2], pages[None, 2:]
    own_shares = finish(products((0,), [out_weight]), (0,), moved[0])
    gate = moved + (own_shares[0], pages_given, pages_kept)

    near = blocks[NEXT]
    moved = weights() + spread(NEXT, own[2:3], NEXT) + spread(NEXT | SIDE, near[:2], SIDE)
    own_shares.update(finish(products((SIDE,), [out_weight]), (SIDE,), moved[0]))
    gate = moved + (own_shares[SIDE],)

    def two_pairs(n):
        return (along[n], across[n], along[n + 1], across[n + 1])

    moved = weights() + spread(NEXT, own[3:], NEXT) + spread(NEXT | SIDE, near[2:3], SIDE)
    pages_side = hop(gated(pages_given), SIDE)
    shares = finish(products((0, SIDE), [two_pairs(0)]), (0, SIDE), moved[0])
    gate = moved + (pages_side, shares[0])

    first_columns = own_columns + far_columns(0, 2)
    moved = weights() + spread(NEXT | SIDE, near[3:], SIDE)
    side_share = jnp.concatenate([own_shares[SIDE], shares[SIDE]], axis=1)
    hand_out(0, own_shares[0], own_columns)
    hand_out(0, shares[0], far_columns(0, 2))
    pages = gated(jnp.concatenate([pages_kept, pages_side], axis=0))
    pages_next = hop(
        lax.dynamic_index_in_dim(pages, 1 - next_here, axis=1, keepdims=False), NEXT
    )
    pages = lax.dynamic_index_in_dim(pages, next_here, axis=1, keepdims=False)
    begun = products((NEXT,), [out_weight, two_pairs(0)])
    shares = finish(begun, (NEXT,))
    begun_near = products((SIDE, NEXT, 0), [after(two_pairs(2), begun[0])])
    gate = moved + (pages_next, begun_near[0])

    moved = weights() + (
        hand_out(NEXT, gated(shares[NEXT]), first_columns),
        hand_out(SIDE, gated(side_share), first_columns),
    )
    pages = gated(jnp.concatenate([pages, pages_next], axis=0))
    limit = data_pages(tok_rows)
    near_lens = pages[:, limit * PAGE, :REQ_INST].astype(jnp.int32)
    far_lens = hop(near_lens, FAR)
    begun = products((NEXT | SIDE,), [out_weight, two_pairs(0), two_pairs(2)])
    near_shares = finish(begun_near, (SIDE, NEXT, 0), begun[0], moved[1])
    far_shares = finish(begun, (NEXT | SIDE,), begun[0], moved[1])
    gate = moved
    for n in range(narrow + 2, len(cuts)):
        moved += weights()
        gate = moved
    far_share = hand_out(
        NEXT | SIDE, far_shares[NEXT | SIDE], own_columns + far_columns(0, 4)
    )
    moved += tuple(
        hand_out(mask, near_shares[mask], far_columns(2, 4)) for mask in (NEXT, SIDE, 0)
    )
    order = [0, SIDE, NEXT, NEXT | SIDE]
    order = order + [at ^ FAR for at in order]
    block_of = jnp.asarray([order.index(i) for i in range(inst_count)], jnp.int32)
    block_of = jnp.take(block_of, jnp.arange(inst_count, dtype=jnp.int32) ^ inst_here)
    lens = jnp.take(jnp.concatenate([near_lens, far_lens], axis=0), block_of, axis=0)
    page_of = slot_pages(lens, placement, page_table, block_of, limit)
    gate = moved + (page_of, far_shares[NEXT | SIDE])

    across.append(swap(gated(along[-1]), "grp"))
    pages_far = hop(gated(pages), FAR)
    masks = (NEXT | SIDE, NEXT, SIDE, 0)
    sums = []
    for n, span in enumerate(spans):
        last = n == len(spans) - 1
        rights = (along[narrow + n], across[narrow + n])
        sums = [
            products(masks, [rights], span, sums, jnp.bfloat16 if last else jnp.float32)
        ]
    sums = sums[0]
    shares = finish(sums, masks, far_share, swaps=2)
    for mask in masks:
        hand_out(mask, shares[mask], far_columns(narrow, narrow + 1))
    projected = place(pieces, segments, offsets, inst_count * own_cols)
    cache = cache_of(
        pages.reshape(-1, kv_width), after(pages_far, projected).reshape(-1, kv_width), page_of
    )
    return (projected, cache)


def solution(mesh):
    return jax.shard_map(
        per_device,
        mesh=mesh,
        in_specs=(
            P(("grp", "inst"), "tp"),
            P(("grp", "inst"), None),
            P("tp", "inst"),
            P(("grp", "inst"), None),
            P("grp"),
            P("grp", None),
        ),
        out_specs=(P(("grp", "inst", "tp"), None), P(("grp", "inst"), None, "tp")),
        check_vma=False,
    )
```

```python
import functools

import jax
import jax.numpy as jnp
from jax import lax
from jax.experimental import pallas as pl
from jax.experimental.pallas import tpu as pltpu
from jax.sharding import PartitionSpec as P

NH = 96
KVH = 8
HD = 128
PAGE = 16
OWNERS = 4
REQ_INST = 4
MAXLEN = 256
QUARTERS = 4
ROWS = 128
LOG2E = 1.4426950408889634

SIDE, NEXT, FAR = 1, 2, 4
MASKS = (0, NEXT, SIDE, NEXT | SIDE)
WIDTH = 128
LIGHT = pl.CostEstimate(flops=0, bytes_accessed=0, transcendentals=0)


def attention_kernel(info, q_ref, k_ref, v_ref, o_ref, *, heads, row_blocks, window):
    for block in range(row_blocks):
        place = info[0] * row_blocks + block
        first = pl.multiple_of(jnp.maximum(place - (window // ROWS - 1), 0) * ROWS, ROWS)
        row = place * ROWS + lax.broadcasted_iota(jnp.int32, (ROWS, window), 0)
        col = first + lax.broadcasted_iota(jnp.int32, (ROWS, window), 1)
        begin = jnp.zeros_like(row)
        for j in range(REQ_INST):
            begin = jnp.where(row >= info[2 + j], info[2 + j], begin)
        bias = jnp.where((col <= row) & (col >= begin), 0.0, -1e30)
        keys = k_ref[pl.ds(first, window), :]
        vals = v_ref[pl.ds(first, window), :]
        vals = jnp.concatenate([vals, jnp.ones_like(vals)], axis=1)
        rows = slice(block * ROWS, (block + 1) * ROWS)
        for head in range(heads):
            cols = slice(head * HD, (head + 1) * HD)
            scores = lax.dot_general(
                q_ref[rows, cols], keys, (((1,), (1,)), ((), ())),
                preferred_element_type=jnp.float32,
            )
            scores = scores * (LOG2E / HD**0.5) + bias
            expo = jnp.exp2(scores - jnp.max(scores, axis=1, keepdims=True))
            mixed = jnp.dot(expo.astype(jnp.bfloat16), vals, preferred_element_type=jnp.float32)
            o_ref[rows, cols] = (mixed[:, :HD] / mixed[:, HD:]).astype(jnp.bfloat16)


def attention(queries, keys_values, ends, first_kv, chunk, chunk_rows, part, parts):
    tok_rows, width = queries.shape
    local_heads = width // HD
    kv_heads = max(1, local_heads // (NH // KVH))
    heads = local_heads // kv_heads
    steps = kv_heads // parts
    window = min(ROWS + MAXLEN, tok_rows)
    first_kv = first_kv + part * steps
    info = jnp.concatenate([jnp.stack([chunk, first_kv]).astype(jnp.int32), ends])
    return pl.pallas_call(
        functools.partial(
            attention_kernel, heads=heads, row_blocks=chunk_rows // ROWS, window=window
        ),
        grid_spec=pltpu.PrefetchScalarGridSpec(
            num_scalar_prefetch=1,
            grid=(steps,),
            in_specs=[
                pl.BlockSpec(
                    (chunk_rows, heads * HD), lambda g, info: (info[0], part * steps + g)
                ),
                pl.BlockSpec((tok_rows, HD), lambda g, info: (0, 2 * (info[1] + g))),
                pl.BlockSpec((tok_rows, HD), lambda g, info: (0, 2 * (info[1] + g) + 1)),
            ],
            out_specs=pl.BlockSpec((chunk_rows, heads * HD), lambda g, info: (0, g)),
        ),
        out_shape=jax.ShapeDtypeStruct((chunk_rows, width // parts), jnp.bfloat16),
        compiler_params=pltpu.CompilerParams(vmem_limit_bytes=60 << 20),
        cost_estimate=LIGHT,
        name="attention",
    )(info, queries, keys_values, keys_values)


def place_kernel(offsets, *refs, segments):
    out = refs[-1]
    for n, (source, at, width) in enumerate(segments):
        start = pl.multiple_of(offsets[n], 128)
        out[:, pl.ds(start, width)] = refs[source][:, at : at + width]


def place(pieces, segments, offsets, columns):
    rows = pieces[0].shape[0]
    block = 64 if rows % 64 == 0 else rows
    return pl.pallas_call(
        functools.partial(place_kernel, segments=segments),
        grid_spec=pltpu.PrefetchScalarGridSpec(
            num_scalar_prefetch=1,
            grid=(rows // block,),
            in_specs=[
                pl.BlockSpec((block, piece.shape[1]), lambda i, offsets: (i, 0))
                for piece in pieces
            ],
            out_specs=pl.BlockSpec((block, columns), lambda i, offsets: (i, 0)),
        ),
        out_shape=jax.ShapeDtypeStruct((rows, columns), pieces[0].dtype),
        compiler_params=pltpu.CompilerParams(vmem_limit_bytes=60 << 20),
        cost_estimate=LIGHT,
        name="place",
    )(jnp.stack(offsets).astype(jnp.int32), *pieces)


def cut_kernel(places, weight_ref, o_ref):
    o_ref[...] = weight_ref[...]


def cut_out(weight, row, height, column, width, block):
    return pl.pallas_call(
        cut_kernel,
        grid_spec=pltpu.PrefetchScalarGridSpec(
            num_scalar_prefetch=1,
            grid=(height // block,),
            in_specs=[pl.BlockSpec((block, width), lambda n, places: (places[0] + n, places[1]))],
            out_specs=pl.BlockSpec((block, width), lambda n, places: (n, 0)),
        ),
        out_shape=jax.ShapeDtypeStruct((height, width), weight.dtype),
        compiler_params=pltpu.CompilerParams(vmem_limit_bytes=60 << 20),
        cost_estimate=LIGHT,
        name="cut",
    )(jnp.stack([jnp.int32(row // block), column // width]).astype(jnp.int32), weight)


def cache_kernel(page_of, pages_ref, o_ref):
    slots = o_ref.shape[0]
    first = pl.program_id(0) * slots
    for n in range(slots):
        page = page_of[first + n]
        start = pl.multiple_of(jnp.maximum(page, 0) * PAGE, PAGE)
        rows = pages_ref[pl.ds(start, PAGE), :]
        o_ref[n] = jnp.where(page >= 0, rows, jnp.zeros_like(rows))


def cache_of(pages, page_of):
    rows, width = pages.shape
    count = page_of.shape[0]
    block = 16 if count % 16 == 0 else count
    return pl.pallas_call(
        cache_kernel,
        grid_spec=pltpu.PrefetchScalarGridSpec(
            num_scalar_prefetch=1,
            grid=(count // block,),
            in_specs=[pl.BlockSpec((rows, width), lambda i, page_of: (0, 0))],
            out_specs=pl.BlockSpec((block, PAGE, width), lambda i, page_of: (i, 0, 0)),
        ),
        out_shape=jax.ShapeDtypeStruct((count, PAGE, width), pages.dtype),
        compiler_params=pltpu.CompilerParams(vmem_limit_bytes=60 << 20),
        cost_estimate=LIGHT,
        name="cache",
    )(page_of, pages)


def hop(array, mask):
    count = lax.axis_size("inst")
    return lax.ppermute(array, "inst", [(i, i ^ mask) for i in range(count)])


def swap(array, axis):
    return lax.ppermute(array, axis, [(0, 1), (1, 0)])


def product_kernel(*refs, masks, chunks, segments, groups, summands):
    step = pl.program_id(0)
    parts = 1 + max(part for part, _, _ in segments)
    count = masks * chunks * parts
    left_refs, rest = refs[:count], refs[count:]
    sources, wide = [], []
    for _, size, _ in groups:
        taken = max(size, 1)
        if size:
            sources.extend(rest[:taken])
        wide.append(None if size else rest[0])
        rest = rest[taken:]
    others, rest = rest[: summands * chunks], rest[summands * chunks :]
    outs, rest = rest[:chunks], rest[chunks:]
    held, rest = rest[: len(sources)], rest[len(sources) :]
    lefts, sems = rest[:-1], rest[-1]
    rows = left_refs[0].shape[0]

    copies, narrow_copies = [], []
    for mask in range(masks):
        mine = []
        for chunk in range(chunks):
            block = mask * chunks + chunk
            for n, (part, start, size) in enumerate(segments):
                mine.append(
                    pltpu.make_async_copy(
                        left_refs[block * parts + part].at[:, start : start + size],
                        lefts[n].at[block * rows : (block + 1) * rows, :],
                        sems.at[block * len(segments) + n],
                    )
                )
        copies.append(mine)
    used = masks * chunks * len(segments)
    for n, ref in enumerate(sources):
        narrow_copies.append(pltpu.make_async_copy(ref, held[n], sems.at[used + n]))

    def start():
        mine = [copy for group in copies for copy in group]
        for copy in narrow_copies + mine if groups[0][1] else mine + narrow_copies:
            copy.start()

    def compute(rights, stacked, arrived, first, alone):
        for copy in arrived:
            copy.wait()
        for mask in range(masks):
            if first == 0:
                for copy in copies[mask]:
                    if alone:
                        copy.wait()
                    else:
                        pl.when(step == 0)(copy.wait)
            total, at = None, 0
            span = slice(mask * chunks * rows, (mask + 1) * chunks * rows)
            for n, (_, _, size) in enumerate(segments):
                if stacked > 1:
                    mine = rights[n * len(rights) // stacked : (n + 1) * len(rights) // stacked]
                    right = jnp.concatenate([ref[...] for ref in mine], axis=1)
                else:
                    right = jnp.concatenate([ref[at : at + size, :] for ref in rights], axis=1)
                term = jnp.dot(lefts[n][span, :], right, preferred_element_type=jnp.float32)
                total = term if total is None else total + term
                at += size
            span = slice(mask * rows, (mask + 1) * rows)
            for chunk in range(chunks):
                result = total[chunk * rows : (chunk + 1) * rows, :]
                for other in others[chunk::chunks]:
                    result = result + other[span, :].astype(jnp.float32)
                outs[chunk][span, :] = result.astype(outs[chunk].dtype)

    if sum(steps for steps, _, _ in groups) == 1:
        start()
    else:
        pl.when(step == 0)(start)
    first, at = 0, 0
    for (steps, size, stacked), ref in zip(groups, wide):
        rights = held[at : at + size] if size else [ref]
        body = functools.partial(
            compute, rights, stacked, narrow_copies[at : at + size], first, steps == 1
        )
        at += size
        if len(groups) == 1:
            body()
        else:
            pl.when((step >= first) & (step < first + steps))(body)
        first += steps


def product(blocks, rights, span, summands=(), dtype=jnp.bfloat16):
    masks, chunks, parts = len(blocks), len(blocks[0]), len(blocks[0][0])
    rows, depth = blocks[0][0][0].shape
    segments = []
    for part in range(parts):
        low, high = max(span[0] - part * depth, 0), min(span[1] - part * depth, depth)
        if low < high:
            segments.append((part, low, high - low))
    skipped = segments[0][0]
    segments = [(part - skipped, low, size) for part, low, size in segments]
    block = 4 * WIDTH
    anywhere = pl.BlockSpec(memory_space=pl.ANY)
    operands = [
        array
        for mask in blocks
        for chunk in mask
        for array in chunk[skipped : skipped + 1 + segments[-1][0]]
    ]
    specs = [anywhere] * len(operands)
    copies = masks * chunks * len(segments)
    groups, held, first = [], [], 0
    for right in rights:
        if isinstance(right, (tuple, list)):
            steps, stacked = 1, 1
            if isinstance(right, list):
                stacked = len(right)
                right = [piece for pieces in right for piece in pieces]
            operands += right
            specs += [anywhere] * len(right)
            held += [pltpu.VMEM(piece.shape, piece.dtype) for piece in right]
            groups.append((1, len(right), stacked))
        else:
            steps = right.shape[1] // block
            operands.append(right)
            specs.append(
                pl.BlockSpec(
                    (right.shape[0], block),
                    lambda n, first=first, steps=steps: (0, jnp.clip(n - first, 0, steps - 1)),
                )
            )
            groups.append((steps, 0, 1))
        first += steps
    out_spec = pl.BlockSpec((rows * masks, block), lambda n: (0, n))
    for summand in summands:
        operands += summand
        specs += [out_spec] * chunks
    scratch = [
        pltpu.VMEM((masks * chunks * rows, size), operands[0].dtype) for _, _, size in segments
    ]
    return pl.pallas_call(
        functools.partial(
            product_kernel, masks=masks, chunks=chunks, segments=segments, groups=groups,
            summands=len(summands),
        ),
        grid=(first,),
        in_specs=specs,
        out_specs=[out_spec] * chunks,
        out_shape=[jax.ShapeDtypeStruct((rows * masks, first * block), dtype)] * chunks,
        scratch_shapes=held + scratch + [pltpu.SemaphoreType.DMA((copies + len(held),))],
        compiler_params=pltpu.CompilerParams(vmem_limit_bytes=60 << 20),
        cost_estimate=LIGHT,
        name="product",
    )(*operands)


def after(array, *earlier):
    return lax.optimization_barrier((array,) + earlier)[0]


def data_pages(tok_rows):
    span = PAGE * OWNERS
    return (tok_rows + REQ_INST * (span - 1)) // span


def packing(lens, residue):
    page_counts = (lens + (PAGE - 1)) // PAGE
    counts = jnp.maximum(page_counts - residue + (OWNERS - 1), 0) // OWNERS
    return counts, jnp.cumsum(counts, axis=-1) - counts


def packed_pages(held, lens, residues, tok_rows):
    limit = data_pages(tok_rows)
    starts = jnp.cumsum(lens) - lens
    residues = jnp.stack(residues)[:, None]
    counts, firsts = packing(lens[None, :], residues)
    slot = jnp.arange(limit + 1, dtype=jnp.int32)
    step = slot[None, :, None] - firsts[:, None, :]
    mine = (step >= 0) & (step < counts[:, None, :])
    offset = (step * OWNERS + residues[:, :, None]) * PAGE
    base = jnp.sum(jnp.where(mine, starts[None, None, :] + offset, 0), axis=2)
    live = jnp.sum(jnp.where(mine, jnp.minimum(lens[None, None, :] - offset, PAGE), 0), axis=2)
    base = jnp.where(slot[None, :] == limit, tok_rows, base)
    live = jnp.where(slot[None, :] == limit, PAGE, live)
    within = jnp.arange(PAGE, dtype=jnp.int32)
    row = jnp.where(
        within[None, None, :] < live[:, :, None], base[:, :, None] + within[None, None, :], -1
    ).reshape(-1)
    chosen = row[:, None] == jnp.arange(held.shape[0], dtype=jnp.int32)[None, :]
    pages = jnp.dot(chosen.astype(held.dtype), held, preferred_element_type=jnp.float32)
    return pages.astype(held.dtype).reshape(residues.shape[0], (limit + 1) * PAGE, held.shape[1])


def slot_pages(lens, placement, page_table, block_of, limit):
    inst_here = lax.axis_index("inst")
    residue = inst_here % OWNERS
    requests = page_table.shape[0]
    slot_count = requests * QUARTERS
    counts, firsts = packing(lens, residue)
    slots = lax.dynamic_index_in_dim(
        page_table.reshape(requests, QUARTERS, OWNERS), residue, axis=2, keepdims=False
    )
    step = jnp.arange(QUARTERS, dtype=jnp.int32)
    valid = (placement == inst_here // OWNERS)[:, None] & (step[None, :] < counts.reshape(-1)[:, None])
    page = (firsts + block_of[:, None] * (limit + 1)).reshape(-1)[:, None] + step[None, :]
    target = jnp.where(valid, slots, slot_count).reshape(-1)
    match = target[None, :] == jnp.arange(slot_count, dtype=jnp.int32)[:, None]
    return jnp.sum(jnp.where(match, page.reshape(-1)[None, :] + 1, 0), axis=1) - 1


def per_device(queries, keys_values, out_weight, lengths, placement, page_table):
    tok_rows = queries.shape[0]
    tp_count = lax.axis_size("tp")
    tp_here = lax.axis_index("tp")
    inst_count = lax.axis_size("inst")
    inst_here = lax.axis_index("inst")
    grp_here = lax.axis_index("grp")
    side_here = inst_here % 2
    next_here = inst_here // NEXT % 2
    local_heads = queries.shape[1] // HD
    first_kv = tp_here * local_heads // (NH // KVH)
    ends = jnp.cumsum(lengths[0])
    depth, own_cols = out_weight.shape
    half_cols = own_cols // 2
    kv_width = keys_values.shape[1] // tp_count

    narrow = 4
    parts = 4 if depth % 512 == 0 else 2
    spans = [(0, depth // 2)] + [
        (n * depth // parts, (n + 1) * depth // parts) for n in range(parts // 2, parts)
    ]
    cuts = [(0, depth, n * WIDTH, WIDTH) for n in range(narrow)] + [
        (low, high - low, narrow * WIDTH, half_cols - narrow * WIDTH) for low, high in spans
    ]

    gate = ()

    def gated(array):
        return after(array, *gate) if gate else array

    def cut(n, *earlier):
        weight = after(out_weight, *earlier) if earlier else out_weight
        row, height, column, width = cuts[n]
        return cut_out(
            weight, row, height, grp_here * half_cols + column, width, depth // parts
        )

    pieces, segments, offsets = [], [], []
    own_columns = [(own_cols, lambda inst: inst * own_cols)]

    def far_columns(first, last):
        return [
            (
                cuts[n][3],
                lambda inst, n=n, half=half: (inst ^ FAR) * own_cols + half * half_cols + cuts[n][2],
            )
            for n in range(first, last)
            for half in (grp_here, 1 - grp_here)
        ]

    def hand_out(mask, share, columns):
        at = 0
        for width, column_of in columns:
            segments.append((len(pieces), at, width))
            offsets.append(column_of(inst_here ^ mask))
            at += width
        pieces.append(hop(share, mask) if mask else share)
        return pieces[-1]

    kv_parts = 2 if local_heads % (2 * (NH // KVH)) == 0 else 1
    blocks = {mask: [] for mask in MASKS}

    def products(masks, rights, span=(0, depth), summands=(), dtype=jnp.bfloat16):
        groups = []
        for mask in masks:
            rows = blocks[mask]
            groups.append([rows[n : n + kv_parts] for n in range(0, len(rows), kv_parts)])
        groups[0][0] = [gated(array) for array in groups[0][0]]
        return product(groups, rights, span, summands, dtype)

    def finish(totals, masks, *earlier):
        given = after(totals[0], *earlier) if earlier else totals[0]
        rows = given.shape[0] // len(masks)
        if tp_count == 2:
            other = swap(given, "tp")
            total = (totals[1].astype(jnp.float32) + other.astype(jnp.float32)).astype(other.dtype)
            return {mask: total[n * rows : (n + 1) * rows] for n, mask in enumerate(masks)}
        return {
            mask: lax.psum_scatter(
                given[n * rows : (n + 1) * rows], "tp", scatter_dimension=0, tiled=True
            )
            for n, mask in enumerate(masks)
        }

    sliced, along, across = [cut(0)], [], []
    along.append(hop(sliced[0], FAR))
    held = lax.dynamic_slice_in_dim(
        after(keys_values, sliced[0]), tp_here * kv_width, kv_width, 1
    )
    lens_rows = jnp.zeros((PAGE, kv_width), held.dtype)
    lens_rows = lens_rows.at[0, :REQ_INST].set(lengths[0].astype(held.dtype))
    held = jnp.concatenate([held, lens_rows], axis=0)
    held_far = hop(held, FAR)
    chunks = [1 - tp_here, tp_here] if tp_count == 2 else [jnp.int32(0)]
    own = blocks[0]
    ready = held
    for chunk in chunks:
        for part in range(kv_parts):
            ready = attention(
                after(queries, ready), keys_values, ends, first_kv, chunk,
                tok_rows // len(chunks), part, kv_parts,
            )
            own.append(ready)

    def spread(name, arrays, mask):
        sent = [hop(gated(array), mask) for array in arrays]
        blocks[name] += sent
        return tuple(sent)

    moved = spread(NEXT, own[:1], NEXT) + spread(SIDE, own[:2], SIDE)
    for n in range(1, len(cuts)):
        ready = cut(n, ready)
        sliced.append(ready)

    seen = jnp.sum(along[0].astype(jnp.float32), axis=0)
    seen_far = jnp.sum(held_far.astype(jnp.float32), axis=0)
    gate = moved + (along[0], held_far, seen, seen_far, ready)

    def weights():
        n = len(across)
        across.append(swap(gated(along[n]), "grp"))
        along.append(hop(gated(sliced[n + 1]), FAR))
        return (across[-1], along[-1])

    moved = weights() + spread(NEXT, own[1:2], NEXT) + spread(SIDE, own[2:], SIDE)
    held_far = gated(held_far)
    pages_given, pages_kept = (
        jnp.stack(
            [
                packed_pages(rows, lens, residues, tok_rows)
                for rows, lens in (
                    (held, lengths[0]),
                    (held_far, held_far[tok_rows, :REQ_INST].astype(jnp.int32)),
                )
            ]
        )
        for residues in ([1 - side_here, 3 - side_here], [side_here, 2 + side_here])
    )
    own_shares = finish(products((0,), [out_weight]), (0,), moved[0])
    gate = moved + (own_shares[0], pages_given, pages_kept)

    near = blocks[NEXT]
    moved = weights() + spread(NEXT, own[2:3], NEXT) + spread(NEXT | SIDE, near[:2], SIDE)
    own_shares.update(finish(products((SIDE,), [out_weight]), (SIDE,), moved[0]))
    gate = moved + (own_shares[SIDE],)

    def two_pairs(n):
        return (along[n], across[n], along[n + 1], across[n + 1])

    moved = weights() + spread(NEXT, own[3:], NEXT) + spread(NEXT | SIDE, near[2:3], SIDE)
    pages_side = hop(gated(pages_given), SIDE)
    shares = finish(products((0, SIDE), [two_pairs(0)]), (0, SIDE), moved[0])
    gate = moved + (pages_side, shares[0])

    first_columns = own_columns + far_columns(0, 2)
    moved = weights() + spread(NEXT | SIDE, near[3:], SIDE)
    side_share = jnp.concatenate([own_shares[SIDE], shares[SIDE]], axis=1)
    hand_out(0, own_shares[0], own_columns)
    hand_out(0, shares[0], far_columns(0, 2))
    pages = gated(jnp.concatenate([pages_kept, pages_side], axis=0))
    pages_next = hop(
        lax.dynamic_index_in_dim(pages, 1 - next_here, axis=1, keepdims=False), NEXT
    )
    pages = lax.dynamic_index_in_dim(pages, next_here, axis=1, keepdims=False)
    begun = products((NEXT,), [out_weight, two_pairs(0)])
    shares = finish(begun, (NEXT,))
    begun_near = products((SIDE, NEXT, 0), [after(two_pairs(2), begun[0])])
    gate = moved + (pages_next, begun_near[0])

    moved = weights() + (
        hand_out(NEXT, gated(shares[NEXT]), first_columns),
        hand_out(SIDE, gated(side_share), first_columns),
    )
    begun = products((NEXT | SIDE,), [out_weight, two_pairs(0), two_pairs(2)])
    near_shares = finish(begun_near, (SIDE, NEXT, 0), begun[0], moved[1])
    far_shares = finish(begun, (NEXT | SIDE,), begun[0], moved[1])
    gate = moved
    for n in range(narrow + 2, len(cuts)):
        moved += weights()
        gate = moved
    far_share = hand_out(
        NEXT | SIDE, far_shares[NEXT | SIDE], own_columns + far_columns(0, 4)
    )
    moved += tuple(
        hand_out(mask, near_shares[mask], far_columns(2, 4)) for mask in (NEXT, SIDE, 0)
    )
    pages = jnp.concatenate([pages, after(pages_next, near_shares[0])], axis=0)
    order = [mask ^ far for mask in (0, SIDE) for far in (0, FAR)]
    order = order + [at ^ NEXT for at in order]
    block_of = jnp.asarray([order.index(i) for i in range(inst_count)], jnp.int32)
    block_of = jnp.take(block_of, jnp.arange(inst_count, dtype=jnp.int32) ^ inst_here)
    limit = data_pages(tok_rows)
    lens = jnp.take(pages[:, limit * PAGE, :REQ_INST].astype(jnp.int32), block_of, axis=0)
    page_of = slot_pages(lens, placement, page_table, block_of, limit)
    cache = cache_of(pages.reshape(-1, kv_width), page_of)
    gate = moved + (cache, far_shares[NEXT | SIDE])

    across.append(swap(gated(along[-1]), "grp"))
    masks = (NEXT | SIDE, NEXT, SIDE, 0)
    far_pairs = [(along[narrow + n], across[narrow + n]) for n in range(len(spans))]
    early = far_pairs[0] if len(spans) == 2 else far_pairs[:-1]
    sums = products(masks, [early], (0, spans[-1][0]))
    gate = (far_share,)
    sums = products(masks, [after(far_pairs[-1], sums[0])], spans[-1], [sums])
    shares = finish(sums, masks)
    for mask in masks:
        hand_out(mask, shares[mask], far_columns(narrow, narrow + 1))
    projected = place(pieces, segments, offsets, inst_count * own_cols)
    return (projected, cache)


def solution(mesh):
    return jax.shard_map(
        per_device,
        mesh=mesh,
        in_specs=(
            P(("grp", "inst"), "tp"),
            P(("grp", "inst"), None),
            P("tp", "inst"),
            P(("grp", "inst"), None),
            P("grp"),
            P("grp", None),
        ),
        out_specs=(P(("grp", "inst", "tp"), None), P(("grp", "inst"), None, "tp")),
        check_vma=False,
    )
```

```python
import functools

import jax
import jax.numpy as jnp
from jax import lax
from jax.experimental import pallas as pl
from jax.experimental.pallas import tpu as pltpu
from jax.sharding import PartitionSpec as P

NH = 96
KVH = 8
HD = 128
PAGE = 16
OWNERS = 4
REQ_INST = 4
MAXLEN = 256
QUARTERS = 4
ROWS = 128
LOG2E = 1.4426950408889634

SIDE, NEXT, FAR = 1, 2, 4
MASKS = (0, NEXT, SIDE, NEXT | SIDE)
WIDTH = 128
LIGHT = pl.CostEstimate(flops=0, bytes_accessed=0, transcendentals=0)


def attention_kernel(info, q_ref, k_ref, v_ref, o_ref, *, heads, row_blocks, window):
    for block in range(row_blocks):
        place = info[0] * row_blocks + block
        first = pl.multiple_of(jnp.maximum(place - (window // ROWS - 1), 0) * ROWS, ROWS)
        row = place * ROWS + lax.broadcasted_iota(jnp.int32, (ROWS, window), 0)
        col = first + lax.broadcasted_iota(jnp.int32, (ROWS, window), 1)
        begin = jnp.zeros_like(row)
        for j in range(REQ_INST):
            begin = jnp.where(row >= info[2 + j], info[2 + j], begin)
        bias = jnp.where((col <= row) & (col >= begin), 0.0, -1e30)
        keys = k_ref[pl.ds(first, window), :]
        vals = v_ref[pl.ds(first, window), :]
        vals = jnp.concatenate([vals, jnp.ones_like(vals)], axis=1)
        rows = slice(block * ROWS, (block + 1) * ROWS)
        for head in range(heads):
            cols = slice(head * HD, (head + 1) * HD)
            scores = lax.dot_general(
                q_ref[rows, cols], keys, (((1,), (1,)), ((), ())),
                preferred_element_type=jnp.float32,
            )
            scores = scores * (LOG2E / HD**0.5) + bias
            expo = jnp.exp2(scores - jnp.max(scores, axis=1, keepdims=True))
            mixed = jnp.dot(expo.astype(jnp.bfloat16), vals, preferred_element_type=jnp.float32)
            o_ref[rows, cols] = (mixed[:, :HD] / mixed[:, HD:]).astype(jnp.bfloat16)


def attention(queries, keys_values, ends, first_kv, chunk, chunk_rows, part, parts):
    tok_rows, width = queries.shape
    local_heads = width // HD
    kv_heads = max(1, local_heads // (NH // KVH))
    heads = local_heads // kv_heads
    steps = kv_heads // parts
    window = min(ROWS + MAXLEN, tok_rows)
    first_kv = first_kv + part * steps
    info = jnp.concatenate([jnp.stack([chunk, first_kv]).astype(jnp.int32), ends])
    return pl.pallas_call(
        functools.partial(
            attention_kernel, heads=heads, row_blocks=chunk_rows // ROWS, window=window
        ),
        grid_spec=pltpu.PrefetchScalarGridSpec(
            num_scalar_prefetch=1,
            grid=(steps,),
            in_specs=[
                pl.BlockSpec(
                    (chunk_rows, heads * HD), lambda g, info: (info[0], part * steps + g)
                ),
                pl.BlockSpec((tok_rows, HD), lambda g, info: (0, 2 * (info[1] + g))),
                pl.BlockSpec((tok_rows, HD), lambda g, info: (0, 2 * (info[1] + g) + 1)),
            ],
            out_specs=pl.BlockSpec((chunk_rows, heads * HD), lambda g, info: (0, g)),
        ),
        out_shape=jax.ShapeDtypeStruct((chunk_rows, width // parts), jnp.bfloat16),
        compiler_params=pltpu.CompilerParams(vmem_limit_bytes=60 << 20),
        cost_estimate=LIGHT,
        name="attention",
    )(info, queries, keys_values, keys_values)


def place_kernel(offsets, *refs, segments):
    out = refs[-1]
    for n, (source, at, width) in enumerate(segments):
        start = pl.multiple_of(offsets[n], 128)
        out[:, pl.ds(start, width)] = refs[source][:, at : at + width]


def place(pieces, segments, offsets, columns):
    rows = pieces[0].shape[0]
    block = 64 if rows % 64 == 0 else rows
    return pl.pallas_call(
        functools.partial(place_kernel, segments=segments),
        grid_spec=pltpu.PrefetchScalarGridSpec(
            num_scalar_prefetch=1,
            grid=(rows // block,),
            in_specs=[
                pl.BlockSpec((block, piece.shape[1]), lambda i, offsets: (i, 0))
                for piece in pieces
            ],
            out_specs=pl.BlockSpec((block, columns), lambda i, offsets: (i, 0)),
        ),
        out_shape=jax.ShapeDtypeStruct((rows, columns), pieces[0].dtype),
        compiler_params=pltpu.CompilerParams(vmem_limit_bytes=60 << 20),
        cost_estimate=LIGHT,
        name="place",
    )(jnp.stack(offsets).astype(jnp.int32), *pieces)


def cut_kernel(places, weight_ref, o_ref):
    o_ref[...] = weight_ref[...]


def cut_out(weight, row, height, column, width, block):
    return pl.pallas_call(
        cut_kernel,
        grid_spec=pltpu.PrefetchScalarGridSpec(
            num_scalar_prefetch=1,
            grid=(height // block,),
            in_specs=[pl.BlockSpec((block, width), lambda n, places: (places[0] + n, places[1]))],
            out_specs=pl.BlockSpec((block, width), lambda n, places: (n, 0)),
        ),
        out_shape=jax.ShapeDtypeStruct((height, width), weight.dtype),
        compiler_params=pltpu.CompilerParams(vmem_limit_bytes=60 << 20),
        cost_estimate=LIGHT,
        name="cut",
    )(jnp.stack([jnp.int32(row // block), column // width]).astype(jnp.int32), weight)


def cache_kernel(page_of, pages_ref, o_ref):
    slots = o_ref.shape[0]
    first = pl.program_id(0) * slots
    for n in range(slots):
        page = page_of[first + n]
        start = pl.multiple_of(jnp.maximum(page, 0) * PAGE, PAGE)
        rows = pages_ref[pl.ds(start, PAGE), :]
        o_ref[n] = jnp.where(page >= 0, rows, jnp.zeros_like(rows))


def cache_of(pages, page_of):
    rows, width = pages.shape
    count = page_of.shape[0]
    block = 16 if count % 16 == 0 else count
    return pl.pallas_call(
        cache_kernel,
        grid_spec=pltpu.PrefetchScalarGridSpec(
            num_scalar_prefetch=1,
            grid=(count // block,),
            in_specs=[pl.BlockSpec((rows, width), lambda i, page_of: (0, 0))],
            out_specs=pl.BlockSpec((block, PAGE, width), lambda i, page_of: (i, 0, 0)),
        ),
        out_shape=jax.ShapeDtypeStruct((count, PAGE, width), pages.dtype),
        compiler_params=pltpu.CompilerParams(vmem_limit_bytes=60 << 20),
        cost_estimate=LIGHT,
        name="cache",
    )(page_of, pages)


def hop(array, mask):
    count = lax.axis_size("inst")
    return lax.ppermute(array, "inst", [(i, i ^ mask) for i in range(count)])


def swap(array, axis):
    return lax.ppermute(array, axis, [(0, 1), (1, 0)])


def product_kernel(*refs, masks, chunks, segments, groups, summands):
    step = pl.program_id(0)
    parts = 1 + max(part for part, _, _ in segments)
    count = masks * chunks * parts
    left_refs, rest = refs[:count], refs[count:]
    sources, wide = [], []
    for _, size, _ in groups:
        taken = max(size, 1)
        if size:
            sources.extend(rest[:taken])
        wide.append(None if size else rest[0])
        rest = rest[taken:]
    others, rest = rest[: summands * chunks], rest[summands * chunks :]
    outs, rest = rest[:chunks], rest[chunks:]
    held, rest = rest[: len(sources)], rest[len(sources) :]
    lefts, sems = rest[:-1], rest[-1]
    rows = left_refs[0].shape[0]

    copies, narrow_copies = [], []
    for mask in range(masks):
        mine = []
        for chunk in range(chunks):
            block = mask * chunks + chunk
            for n, (part, start, size) in enumerate(segments):
                mine.append(
                    pltpu.make_async_copy(
                        left_refs[block * parts + part].at[:, start : start + size],
                        lefts[n].at[block * rows : (block + 1) * rows, :],
                        sems.at[block * len(segments) + n],
                    )
                )
        copies.append(mine)
    used = masks * chunks * len(segments)
    for n, ref in enumerate(sources):
        narrow_copies.append(pltpu.make_async_copy(ref, held[n], sems.at[used + n]))

    def start():
        mine = [copy for group in copies for copy in group]
        for copy in narrow_copies + mine if groups[0][1] else mine + narrow_copies:
            copy.start()

    def compute(rights, stacked, arrived, first, alone):
        for copy in arrived:
            copy.wait()
        for mask in range(masks):
            if first == 0:
                for copy in copies[mask]:
                    if alone:
                        copy.wait()
                    else:
                        pl.when(step == 0)(copy.wait)
            total, at = None, 0
            span = slice(mask * chunks * rows, (mask + 1) * chunks * rows)
            for n, (_, _, size) in enumerate(segments):
                if stacked > 1:
                    mine = rights[n * len(rights) // stacked : (n + 1) * len(rights) // stacked]
                    right = jnp.concatenate([ref[...] for ref in mine], axis=1)
                else:
                    right = jnp.concatenate([ref[at : at + size, :] for ref in rights], axis=1)
                term = jnp.dot(lefts[n][span, :], right, preferred_element_type=jnp.float32)
                total = term if total is None else total + term
                at += size
            span = slice(mask * rows, (mask + 1) * rows)
            for chunk in range(chunks):
                result = total[chunk * rows : (chunk + 1) * rows, :]
                for other in others[chunk::chunks]:
                    result = result + other[span, :].astype(jnp.float32)
                outs[chunk][span, :] = result.astype(outs[chunk].dtype)

    if sum(steps for steps, _, _ in groups) == 1:
        start()
    else:
        pl.when(step == 0)(start)
    first, at = 0, 0
    for (steps, size, stacked), ref in zip(groups, wide):
        rights = held[at : at + size] if size else [ref]
        body = functools.partial(
            compute, rights, stacked, narrow_copies[at : at + size], first, steps == 1
        )
        at += size
        if len(groups) == 1:
            body()
        else:
            pl.when((step >= first) & (step < first + steps))(body)
        first += steps


def product(blocks, rights, span, summands=(), dtype=jnp.bfloat16):
    masks, chunks, parts = len(blocks), len(blocks[0]), len(blocks[0][0])
    rows, depth = blocks[0][0][0].shape
    segments = []
    for part in range(parts):
        low, high = max(span[0] - part * depth, 0), min(span[1] - part * depth, depth)
        if low < high:
            segments.append((part, low, high - low))
    skipped = segments[0][0]
    segments = [(part - skipped, low, size) for part, low, size in segments]
    block = 4 * WIDTH
    anywhere = pl.BlockSpec(memory_space=pl.ANY)
    operands = [
        array
        for mask in blocks
        for chunk in mask
        for array in chunk[skipped : skipped + 1 + segments[-1][0]]
    ]
    specs = [anywhere] * len(operands)
    copies = masks * chunks * len(segments)
    groups, held, first = [], [], 0
    for right in rights:
        if isinstance(right, (tuple, list)):
            steps, stacked = 1, 1
            if isinstance(right, list):
                stacked = len(right)
                right = [piece for pieces in right for piece in pieces]
            operands += right
            specs += [anywhere] * len(right)
            held += [pltpu.VMEM(piece.shape, piece.dtype) for piece in right]
            groups.append((1, len(right), stacked))
        else:
            steps = right.shape[1] // block
            operands.append(right)
            specs.append(
                pl.BlockSpec(
                    (right.shape[0], block),
                    lambda n, first=first, steps=steps: (0, jnp.clip(n - first, 0, steps - 1)),
                )
            )
            groups.append((steps, 0, 1))
        first += steps
    out_spec = pl.BlockSpec((rows * masks, block), lambda n: (0, n))
    for summand in summands:
        operands += summand
        specs += [out_spec] * chunks
    scratch = [
        pltpu.VMEM((masks * chunks * rows, size), operands[0].dtype) for _, _, size in segments
    ]
    return pl.pallas_call(
        functools.partial(
            product_kernel, masks=masks, chunks=chunks, segments=segments, groups=groups,
            summands=len(summands),
        ),
        grid=(first,),
        in_specs=specs,
        out_specs=[out_spec] * chunks,
        out_shape=[jax.ShapeDtypeStruct((rows * masks, first * block), dtype)] * chunks,
        scratch_shapes=held + scratch + [pltpu.SemaphoreType.DMA((copies + len(held),))],
        compiler_params=pltpu.CompilerParams(vmem_limit_bytes=60 << 20),
        cost_estimate=LIGHT,
        name="product",
    )(*operands)


def after(array, *earlier):
    return lax.optimization_barrier((array,) + earlier)[0]


def data_pages(tok_rows):
    span = PAGE * OWNERS
    return (tok_rows + REQ_INST * (span - 1)) // span


def packing(lens, residue):
    page_counts = (lens + (PAGE - 1)) // PAGE
    counts = jnp.maximum(page_counts - residue + (OWNERS - 1), 0) // OWNERS
    return counts, jnp.cumsum(counts, axis=-1) - counts


def packed_pages(held, lens, residues, tok_rows):
    limit = data_pages(tok_rows)
    starts = jnp.cumsum(lens) - lens
    residues = jnp.stack(residues)[:, None]
    counts, firsts = packing(lens[None, :], residues)
    slot = jnp.arange(limit + 1, dtype=jnp.int32)
    step = slot[None, :, None] - firsts[:, None, :]
    mine = (step >= 0) & (step < counts[:, None, :])
    offset = (step * OWNERS + residues[:, :, None]) * PAGE
    base = jnp.sum(jnp.where(mine, starts[None, None, :] + offset, 0), axis=2)
    live = jnp.sum(jnp.where(mine, jnp.minimum(lens[None, None, :] - offset, PAGE), 0), axis=2)
    base = jnp.where(slot[None, :] == limit, tok_rows, base)
    live = jnp.where(slot[None, :] == limit, PAGE, live)
    within = jnp.arange(PAGE, dtype=jnp.int32)
    row = jnp.where(
        within[None, None, :] < live[:, :, None], base[:, :, None] + within[None, None, :], -1
    ).reshape(-1)
    chosen = row[:, None] == jnp.arange(held.shape[0], dtype=jnp.int32)[None, :]
    pages = jnp.dot(chosen.astype(held.dtype), held, preferred_element_type=jnp.float32)
    return pages.astype(held.dtype).reshape(residues.shape[0], (limit + 1) * PAGE, held.shape[1])


def slot_pages(lens, placement, page_table, block_of, limit):
    inst_here = lax.axis_index("inst")
    residue = inst_here % OWNERS
    requests = page_table.shape[0]
    slot_count = requests * QUARTERS
    counts, firsts = packing(lens, residue)
    slots = lax.dynamic_index_in_dim(
        page_table.reshape(requests, QUARTERS, OWNERS), residue, axis=2, keepdims=False
    )
    step = jnp.arange(QUARTERS, dtype=jnp.int32)
    valid = (placement == inst_here // OWNERS)[:, None] & (step[None, :] < counts.reshape(-1)[:, None])
    page = (firsts + block_of[:, None] * (limit + 1)).reshape(-1)[:, None] + step[None, :]
    target = jnp.where(valid, slots, slot_count).reshape(-1)
    match = target[None, :] == jnp.arange(slot_count, dtype=jnp.int32)[:, None]
    return jnp.sum(jnp.where(match, page.reshape(-1)[None, :] + 1, 0), axis=1) - 1


def per_device(queries, keys_values, out_weight, lengths, placement, page_table):
    tok_rows = queries.shape[0]
    tp_count = lax.axis_size("tp")
    tp_here = lax.axis_index("tp")
    inst_count = lax.axis_size("inst")
    inst_here = lax.axis_index("inst")
    grp_here = lax.axis_index("grp")
    side_here = inst_here % 2
    next_here = inst_here // NEXT % 2
    local_heads = queries.shape[1] // HD
    first_kv = tp_here * local_heads // (NH // KVH)
    ends = jnp.cumsum(lengths[0])
    depth, own_cols = out_weight.shape
    half_cols = own_cols // 2
    kv_width = keys_values.shape[1] // tp_count

    narrow = 4
    parts = 4 if depth % 512 == 0 else 2
    spans = [(0, depth // 2)] + [
        (n * depth // parts, (n + 1) * depth // parts) for n in range(parts // 2, parts)
    ]
    cuts = [(0, depth, n * WIDTH, WIDTH) for n in range(narrow)] + [
        (low, high - low, narrow * WIDTH, half_cols - narrow * WIDTH) for low, high in spans
    ]

    gate = ()

    def gated(array):
        return after(array, *gate) if gate else array

    def cut(n, *earlier):
        weight = after(out_weight, *earlier) if earlier else out_weight
        row, height, column, width = cuts[n]
        return cut_out(
            weight, row, height, grp_here * half_cols + column, width, depth // parts
        )

    pieces, segments, offsets = [], [], []
    own_columns = [(own_cols, lambda inst: inst * own_cols)]

    def far_columns(first, last):
        return [
            (
                cuts[n][3],
                lambda inst, n=n, half=half: (inst ^ FAR) * own_cols + half * half_cols + cuts[n][2],
            )
            for n in range(first, last)
            for half in (grp_here, 1 - grp_here)
        ]

    def hand_out(mask, share, columns):
        at = 0
        for width, column_of in columns:
            segments.append((len(pieces), at, width))
            offsets.append(column_of(inst_here ^ mask))
            at += width
        pieces.append(hop(share, mask) if mask else share)
        return pieces[-1]

    kv_parts = 2 if local_heads % (2 * (NH // KVH)) == 0 else 1
    blocks = {mask: [] for mask in MASKS}

    def products(masks, rights, span=(0, depth), summands=(), dtype=jnp.bfloat16):
        groups = []
        for mask in masks:
            rows = blocks[mask]
            groups.append([rows[n : n + kv_parts] for n in range(0, len(rows), kv_parts)])
        groups[0][0] = [gated(array) for array in groups[0][0]]
        return product(groups, rights, span, summands, dtype)

    def finish(totals, masks, *earlier):
        given = after(totals[0], *earlier) if earlier else totals[0]
        rows = given.shape[0] // len(masks)
        if tp_count == 2:
            other = swap(given, "tp")
            total = (totals[1].astype(jnp.float32) + other.astype(jnp.float32)).astype(other.dtype)
            return {mask: total[n * rows : (n + 1) * rows] for n, mask in enumerate(masks)}
        return {
            mask: lax.psum_scatter(
                given[n * rows : (n + 1) * rows], "tp", scatter_dimension=0, tiled=True
            )
            for n, mask in enumerate(masks)
        }

    sliced, along, across = [cut(0)], [], []
    along.append(hop(sliced[0], FAR))
    held = lax.dynamic_slice_in_dim(
        after(keys_values, sliced[0]), tp_here * kv_width, kv_width, 1
    )
    lens_rows = jnp.zeros((PAGE, kv_width), held.dtype)
    lens_rows = lens_rows.at[0, :REQ_INST].set(lengths[0].astype(held.dtype))
    held = jnp.concatenate([held, lens_rows], axis=0)
    held_far = hop(held, FAR)
    chunks = [1 - tp_here, tp_here] if tp_count == 2 else [jnp.int32(0)]
    own = blocks[0]
    ready = held
    for chunk in chunks:
        for part in range(kv_parts):
            ready = attention(
                after(queries, ready), keys_values, ends, first_kv, chunk,
                tok_rows // len(chunks), part, kv_parts,
            )
            own.append(ready)

    def spread(name, arrays, mask):
        sent = [hop(gated(array), mask) for array in arrays]
        blocks[name] += sent
        return tuple(sent)

    moved = spread(NEXT, own[:1], NEXT) + spread(SIDE, own[:2], SIDE)
    for n in range(1, len(cuts)):
        ready = cut(n, ready)
        sliced.append(ready)

    seen = jnp.sum(along[0].astype(jnp.float32), axis=0)
    seen_far = jnp.sum(held_far.astype(jnp.float32), axis=0)
    gate = moved + (along[0], held_far, seen, seen_far, ready)

    def weights():
        n = len(across)
        across.append(swap(gated(along[n]), "grp"))
        along.append(hop(gated(sliced[n + 1]), FAR))
        return (across[-1], along[-1])

    moved = weights() + spread(NEXT, own[1:2], NEXT) + spread(SIDE, own[2:], SIDE)
    held_far = gated(held_far)
    pages_given, pages_kept = (
        jnp.stack(
            [
                packed_pages(rows, lens, residues, tok_rows)
                for rows, lens in (
                    (held, lengths[0]),
                    (held_far, held_far[tok_rows, :REQ_INST].astype(jnp.int32)),
                )
            ]
        )
        for residues in ([1 - side_here, 3 - side_here], [side_here, 2 + side_here])
    )
    gate += (pages_given, pages_kept)
    own_shares = finish(products((0,), [out_weight]), (0,), moved[0])
    gate = moved + (own_shares[0],)

    near = blocks[NEXT]
    moved = weights() + spread(NEXT, own[2:3], NEXT) + spread(NEXT | SIDE, near[:2], SIDE)
    own_shares.update(finish(products((SIDE,), [out_weight]), (SIDE,), moved[0]))
    gate = moved + (own_shares[SIDE],)

    def two_pairs(n):
        return (along[n], across[n], along[n + 1], across[n + 1])

    moved = weights() + spread(NEXT, own[3:], NEXT) + spread(NEXT | SIDE, near[2:3], SIDE)
    pages_side = hop(gated(pages_given), SIDE)
    shares = finish(products((0, SIDE), [two_pairs(0)]), (0, SIDE), moved[0])
    gate = moved + (pages_side, shares[0])

    first_columns = own_columns + far_columns(0, 2)
    moved = weights() + spread(NEXT | SIDE, near[3:], SIDE)
    side_share = jnp.concatenate([own_shares[SIDE], shares[SIDE]], axis=1)
    hand_out(0, own_shares[0], own_columns)
    hand_out(0, shares[0], far_columns(0, 2))
    pages = gated(jnp.concatenate([pages_kept, pages_side], axis=0))
    pages_next = hop(
        lax.dynamic_index_in_dim(pages, 1 - next_here, axis=1, keepdims=False), NEXT
    )
    pages = lax.dynamic_index_in_dim(pages, next_here, axis=1, keepdims=False)
    begun = products((NEXT,), [out_weight, two_pairs(0)])
    shares = finish(begun, (NEXT,))
    begun_near = products((SIDE, NEXT, 0), [after(two_pairs(2), begun[0])])
    gate = moved + (pages_next, begun_near[0])

    moved = weights() + (
        hand_out(NEXT, gated(shares[NEXT]), first_columns),
        hand_out(SIDE, gated(side_share), first_columns),
    )
    begun = products((NEXT | SIDE,), [out_weight, two_pairs(0), two_pairs(2)])
    near_shares = finish(begun_near, (SIDE, NEXT, 0), begun[0], moved[1])
    far_shares = finish(begun, (NEXT | SIDE,), begun[0], moved[1])
    gate = moved
    for n in range(narrow + 2, len(cuts)):
        moved += weights()
        gate = moved
    far_share = hand_out(
        NEXT | SIDE, far_shares[NEXT | SIDE], own_columns + far_columns(0, 4)
    )
    moved += tuple(
        hand_out(mask, near_shares[mask], far_columns(2, 4)) for mask in (NEXT, SIDE, 0)
    )
    pages = jnp.concatenate([pages, after(pages_next, near_shares[0])], axis=0)
    order = [mask ^ far for mask in (0, SIDE) for far in (0, FAR)]
    order = order + [at ^ NEXT for at in order]
    block_of = jnp.asarray([order.index(i) for i in range(inst_count)], jnp.int32)
    block_of = jnp.take(block_of, jnp.arange(inst_count, dtype=jnp.int32) ^ inst_here)
    limit = data_pages(tok_rows)
    lens = jnp.take(pages[:, limit * PAGE, :REQ_INST].astype(jnp.int32), block_of, axis=0)
    page_of = slot_pages(lens, placement, page_table, block_of, limit)
    cache = cache_of(pages.reshape(-1, kv_width), page_of)
    gate = moved + (cache, far_shares[NEXT | SIDE])

    across.append(swap(gated(along[-1]), "grp"))
    masks = (NEXT | SIDE, NEXT, SIDE, 0)
    far_pairs = [(along[narrow + n], across[narrow + n]) for n in range(len(spans))]
    early = far_pairs[0] if len(spans) == 2 else far_pairs[:-1]
    sums = products(masks, [early], (0, spans[-1][0]))
    gate = (far_share,)
    sums = products(masks, [after(far_pairs[-1], sums[0])], spans[-1], [sums])
    shares = finish(sums, masks)
    for mask in masks:
        hand_out(mask, shares[mask], far_columns(narrow, narrow + 1))
    projected = place(pieces, segments, offsets, inst_count * own_cols)
    return (projected, cache)


def solution(mesh):
    return jax.shard_map(
        per_device,
        mesh=mesh,
        in_specs=(
            P(("grp", "inst"), "tp"),
            P(("grp", "inst"), None),
            P("tp", "inst"),
            P(("grp", "inst"), None),
            P("grp"),
            P("grp", None),
        ),
        out_specs=(P(("grp", "inst", "tp"), None), P(("grp", "inst"), None, "tp")),
        check_vma=False,
    )
```
